128 devices in a mesh: lat: 4 (over y), lon: 32 (over x, z, core).
Axes of the slice: x: 4, y: 4, z: 4, core: 2. Of those that a mesh axis runs over, the one named last changes fastest.
Arguments:
- footprints: bfloat16 [1536, 12, 128, 512], P(('lat', 'lon')), may hold values from -0.25 to 0.25
- tile_lists: int32 [1536, 12], P(('lat', 'lon')), may hold values from 0 to 16383, as said below
- tile_counts: int32 [1536], P(('lat', 'lon')), may hold values from 6 to 12
- tile_place: int32 [16384], replicated, may hold values from 0 to 16383, as said below
- probes: float32 [1536, 8, 128], P(('lat', 'lon')), may hold values from -6 to 6
- obs_precision: float32 [1536, 128], P(('lat', 'lon')), may hold values from 0.2 to 5
- prior_sigma: float32 [1024, 2048], P('lat', 'lon'), may hold values from 0.3 to 3
- land_mask: int32 [1024, 2048], P('lat', 'lon'), may hold values 0 or 1
Outputs:
- predicted: float32 [1536, 8, 128], P(('lat', 'lon'))
- increment: float32 [1024, 32, 2048], P('lat', None, 'lon')
The draws below stay inside these ranges and needn't reach their ends.
Inputs may be any that keep to these rules, and one draw needn't show every extreme that they name: `tile_lists`: slots j >= tile_counts[g] are padding and are ignored. Grid tile t is held by the device at lat (t // 128) // 32, lon (t % 128) // 4. At most 2 live slots of one device's groups name tiles held by any one device, and one designated device's tiles are named by exactly 2 live slots of every device's groups. `tile_place`: A permutation.
All inputs are finite; a program needn't handle non-finite values. No bound on the sum of `land_mask` on one device may be relied on, other than what follows from the above.
Results may differ from the reference program's by a relative error of at most 0.0034.
Values may be sent and summed in bfloat16 or wider, within the bound.
No kernel may reach another device: no remote copies, remote signals or barrier semaphores. Data moves between devices by JAX's collectives and lax.ppermute only.
A program may use at most 128 MiB of HBM per device.

```python
import math
import jax
import jax.numpy as jnp
from jax import lax

TILE_ROWS = 8
TILE_COLS = 16
WEEKS = 4
PROBES = 8
G = 128
MAXT = 12
NSTEP = 4
CLAT = 256
CLON = 64
SG = 12
CELLS = 128
NLAT = 1024
NLONC = 2048
NTC = 128
NTILES = 16384
NG = 1536
CAP = 2
N_LON = 32
DEVICES = 128


def place_table(key):
    return jax.random.permutation(jax.random.fold_in(key, 103), NTILES).astype(jnp.int32)


def owner_plan(key):
    designated = jax.random.randint(jax.random.fold_in(key, 101), (), 0, DEVICES)
    starred = jax.random.randint(jax.random.fold_in(key, 102), (DEVICES,), 0, SG)
    return (designated, starred)


def draw_tile_place(key, part):
    return place_table(key)


def draw_tile_lists(key, part):
    place = place_table(key)
    designated, starred = owner_plan(key)
    key = jax.random.fold_in(key, 2)
    inverse = jnp.zeros((NTILES,), jnp.int32).at[place].set(jnp.arange(NTILES, dtype=jnp.int32))
    blocks = SG * MAXT
    others = jnp.arange(DEVICES - 1, dtype=jnp.int32)
    others = jnp.where(others >= designated, others + 1, others)
    pool = jnp.tile(others, CAP)

    def one_device(device_key, star):
        shuffled = jax.random.permutation(device_key, pool)
        index = jnp.arange(blocks, dtype=jnp.int32)
        in_run = (index // MAXT == star) & (index % MAXT < CAP)
        ranks = jnp.cumsum(1 - in_run.astype(jnp.int32)) - 1
        picked = shuffled[jnp.clip(ranks, 0, pool.shape[0] - 1)]
        return jnp.where(in_run, designated, picked)
    device_keys = jax.random.split(jax.random.fold_in(key, 3), DEVICES)
    owners = jax.vmap(one_device)(device_keys, starred)
    across = CLON // TILE_COLS
    down = CLAT // TILE_ROWS
    local = jax.random.randint(jax.random.fold_in(key, 4), (DEVICES, blocks), 0, down * across)
    tile_row = owners // N_LON * down + local // across
    tile_col = owners % N_LON * across + local % across
    return inverse[tile_row * NTC + tile_col].reshape(NG, MAXT)


def draw_tile_counts(key, part):
    designated, starred = owner_plan(key)
    key = jax.random.fold_in(key, 5)
    counts = jax.random.randint(key, (DEVICES, SG), max(2, MAXT // 2), MAXT + 1)
    counts = jnp.where(jnp.arange(SG)[None, :] == starred[:, None], MAXT, counts)
    return counts.reshape(NG).astype(jnp.int32)


def with_ends(drawn, key, least, largest):
    longest = drawn.shape.index(max(drawn.shape))
    spots = []
    for shift in (0, 1):
        where = [jax.random.randint(jax.random.fold_in(key, axis), (), 0, length) for axis, length in enumerate(drawn.shape)]
        where[longest] = (where[longest] + shift) % drawn.shape[longest]
        spots.append(tuple(where))
    return drawn.at[spots[0]].set(least).at[spots[1]].set(largest)


def levels(stream_key, extent, cuts, smallest, high):
    loudness = 1.0
    for axis_at, shards_of in cuts:
        heights = jax.random.uniform(jax.random.fold_in(jax.random.fold_in(stream_key, 6), axis_at), (shards_of,), jnp.float32, smallest / len(cuts), high / len(cuts))
        loudness = loudness * jnp.repeat(jnp.exp(heights), extent[axis_at] // shards_of).reshape((-1,) + (1,) * (len(extent) - 1 - axis_at))
    return loudness


def normal_values(rng, extent, deviation, bound, cuts=(), held_as=jnp.bfloat16):
    drawn = jax.random.normal(rng, extent, jnp.float32) * deviation
    if len(cuts) > 0:
        drawn = levels(rng, extent, cuts, -0.22, 0.18) * drawn
    return jnp.clip(drawn, min=-bound, max=bound).astype(held_as)


def setup_inputs(seed: int = 0) -> dict:
    splits = jax.random.split(jax.random.key(seed), 9)
    footprints = normal_values(splits[0], (NG, MAXT, G, WEEKS * CELLS), (WEEKS * G) ** -0.5, 0.25, ((0, 128),))
    tile_lists = draw_tile_lists(jax.random.fold_in(splits[8], 71), 0)
    tile_counts = draw_tile_counts(jax.random.fold_in(splits[8], 71), 0)
    tile_place = draw_tile_place(jax.random.fold_in(splits[8], 71), 0)
    probes = normal_values(splits[4], (NG, PROBES, G), 1.0, 6.0, ((0, 128),), jnp.float32)
    obs_precision = jnp.clip(jnp.exp(math.log(5.0) - 3.218876 * jax.random.uniform(splits[5], (NG, G), jnp.float32) ** levels(splits[5], (NG, G), ((0, 128),), -0.2, 0.2)), 0.2, 5.0)
    prior_sigma = jnp.clip(jnp.exp(math.log(3.0) - 2.3025851 * jax.random.uniform(splits[6], (NLAT, NLONC), jnp.float32) ** levels(splits[6], (NLAT, NLONC), ((0, 4), (1, 32)), -0.2, 0.2)), 0.3, 3.0)
    land_mask = with_ends((jax.random.randint(splits[7], (NLAT, NLONC), 0, 4) < 3).astype(jnp.int32), jax.random.fold_in(splits[7], 1), 0, 1)
    return {"footprints": footprints, "tile_lists": tile_lists, "tile_counts": tile_counts, "tile_place": tile_place, "probes": probes, "obs_precision": obs_precision, "prior_sigma": prior_sigma, "land_mask": land_mask}


diffusion_rate = 0.2
week_decay = 0.6


def diffuse(field):
    for step in range(NSTEP):
        padded = jnp.pad(field, ((1, 1), (0, 0), (1, 1)))
        beside = padded[2:, :, 1:-1] + padded[:-2, :, 1:-1] + padded[1:-1, :, 2:] + padded[1:-1, :, :-2]
        field = field + diffusion_rate * (beside - 4.0 * field)
    return field


def reference(footprints, tile_lists, tile_counts, tile_place, probes, obs_precision, prior_sigma, land_mask):
    flat = PROBES * WEEKS * CELLS
    batches = NG // SG
    tile_grid_rows = NLAT // TILE_ROWS
    weighted = (obs_precision[:, None, :] * probes).astype(jnp.bfloat16)
    live = jnp.arange(MAXT, dtype=jnp.int32)[None, :] < tile_counts[:, None]
    grid_tile = tile_place[tile_lists]
    foot_b = footprints.reshape(batches, SG, MAXT, G, WEEKS * CELLS)
    weight_b = weighted.reshape(batches, SG, PROBES, G)
    tile_b = grid_tile.reshape(batches, SG, MAXT)
    live_b = live.reshape(batches, SG, MAXT)

    def adjoint_step(total, items):
        foot, weight, tiles, alive = items
        part = jnp.einsum("gps,gjsk->gjpk", weight.astype(jnp.float32), foot.astype(jnp.float32),
                          precision=lax.Precision.HIGHEST)
        part = jnp.where(alive[:, :, None, None], part, 0.0)
        return total.at[tiles.reshape(-1)].add(part.reshape(-1, flat)), None

    start = jnp.zeros((NTILES, flat), jnp.float32)
    adjoint, unused = lax.scan(adjoint_step, start, (foot_b, weight_b, tile_b, live_b))
    field = adjoint.reshape(tile_grid_rows, NTC, PROBES * WEEKS, TILE_ROWS, TILE_COLS)
    field = field.transpose(0, 3, 2, 1, 4).reshape(NLAT, PROBES * WEEKS, NLONC)
    scale = prior_sigma * land_mask.astype(jnp.float32)
    scaled = scale[:, None, :] * field
    weeks = jnp.arange(WEEKS, dtype=jnp.float32)
    week_mix = week_decay ** jnp.abs(weeks[:, None] - weeks[None, :])
    mixed = jnp.einsum("wv,lpvc->lpwc", week_mix, scaled.reshape(NLAT, PROBES, WEEKS, NLONC),
                       precision=lax.Precision.HIGHEST).reshape(NLAT, PROBES * WEEKS, NLONC)
    mixed = diffuse(mixed)
    increment = scale[:, None, :] * mixed
    half = increment.astype(jnp.bfloat16)
    tiles_all = half.reshape(tile_grid_rows, TILE_ROWS, PROBES * WEEKS, NTC, TILE_COLS)
    tiles_all = tiles_all.transpose(0, 3, 2, 1, 4).reshape(NTILES, PROBES, WEEKS * CELLS)

    def forward_step(items):
        foot, tiles, alive = items
        blocks = tiles_all[tiles]
        value = jnp.einsum("gjpk,gjsk->gjps", blocks.astype(jnp.float32), foot.astype(jnp.float32),
                           precision=lax.Precision.HIGHEST)
        return jnp.sum(jnp.where(alive[:, :, None, None], value, 0.0), axis=1)

    predicted = lax.map(forward_step, (foot_b, tile_b, live_b)).reshape(NG, PROBES, G)
    return predicted, increment
```

```python
import functools

import jax
import jax.numpy as jnp
import numpy as np
from jax import lax
from jax.experimental import pallas as pl
from jax.experimental.pallas import tpu as pltpu
from jax.sharding import PartitionSpec as P

TILE_ROWS = 8
TILE_COLS = 16
WEEKS = 4
PROBES = 8
NSTEP = 4
CELLS = 128
SLOT_ROWS = WEEKS * PROBES
DOWN = 32
ACROSS = 4
TILES = DOWN * ACROSS

diffusion_rate = 0.2
week_decay = 0.6
MIB = 1 << 20

STEP_FACTOR = diffusion_rate**NSTEP


def stencil_coefficients():
    out = np.zeros((9, 9), np.int64)
    out[4, 4] = 1
    for _ in range(NSTEP):
        padded = np.pad(out, 1)
        out = (
            padded[1:-1, 1:-1]
            + padded[2:, 1:-1]
            + padded[:-2, 1:-1]
            + padded[1:-1, 2:]
            + padded[1:-1, :-2]
        )
    return out


def stencil_weights():
    coef = stencil_coefficients()
    lane = np.arange(128)
    r, c = lane // 16, lane % 16
    rows_own = r
    rows_ns = np.where(r < 4, 8 + r, r - 8)
    cols_ew = np.where(c < 8, 32 + c, c - 16)
    row_in = np.concatenate([rows_own] * 3 + [rows_ns] * 3)
    col_in = np.concatenate([c, 16 + c, cols_ew] * 2)
    row_out = np.concatenate([r, r])
    col_out = np.concatenate([c, 16 + c])
    dr = row_in[:, None] - row_out[None, :]
    dc = col_in[:, None] - col_out[None, :]
    near = (np.abs(dr) <= 4) & (np.abs(dc) <= 4)
    return np.where(near, coef[np.clip(dr + 4, 0, 8), np.clip(dc + 4, 0, 8)], 0).astype(np.float32)


def reflections():
    out = np.zeros((4, 128, 128), np.float32)
    for k in range(1, 4):
        for c in range(16):
            out[0, (k - 1) * 16 + c, (7 - k) * 16 + c] = -1
            out[1, (8 - k) * 16 + c, k * 16 + c] = -1
        for r in range(8):
            out[2, r * 16 + k - 1, r * 16 + 15 - k] = -1
            out[3, r * 16 + 16 - k, r * 16 + k] = -1
    return out


def adjoint_kernel(tile_ref, count_ref, probe_ref, prec_ref, foot_ref, out_ref, table_ref, pos_ref, seen_ref):
    g = pl.program_id(0)
    slots = foot_ref.shape[1]

    @pl.when(g == 0)
    def _():
        def clear(i, carry):
            table_ref[2 * i] = TILES
            table_ref[2 * i + 1] = TILES
            seen_ref[i] = 0
            return carry

        lax.fori_loop(0, 128, clear, 0, unroll=8)

    weighted = (prec_ref[pl.ds(g, 1), :] * probe_ref[0]).astype(jnp.bfloat16)
    count = count_ref[g]

    def slot(j):
        t = tile_ref[g * slots + j]
        row = lax.shift_right_logical(t, 7)
        col = jnp.bitwise_and(t, 127)
        owner = lax.shift_right_logical(row, 5) * 32 + lax.shift_right_logical(col, 2)
        local = jnp.bitwise_and(col, 3) * DOWN + jnp.bitwise_and(row, 31)
        rank = jnp.minimum(seen_ref[owner], 1)
        seen_ref[owner] = rank + 1
        place = owner * 2 + rank
        table_ref[place] = local
        pos_ref[g * slots + j] = place
        part = jnp.dot(weighted, foot_ref[0, j], preferred_element_type=jnp.float32)
        part = jnp.concatenate([part[:, w * CELLS : (w + 1) * CELLS] for w in range(WEEKS)], axis=0)
        out_ref[owner, pl.ds(pl.multiple_of(rank * SLOT_ROWS, SLOT_ROWS), SLOT_ROWS), :] = part.astype(jnp.bfloat16)

    for j in range(slots):
        if j < 6:
            slot(j)
        else:

            @pl.when(j < count)
            def _():
                slot(j)

            @pl.when(j >= count)
            def _():
                pos_ref[g * slots + j] = 0


def adjoint_call(grid_tile, counts, probes, precision, footprints):
    groups, slots, sounds, span = footprints.shape
    return pl.pallas_call(
        adjoint_kernel,
        out_shape=(
            jax.ShapeDtypeStruct((128, 2 * SLOT_ROWS, CELLS), jnp.bfloat16),
            jax.ShapeDtypeStruct((256,), jnp.int32),
            jax.ShapeDtypeStruct((groups * slots,), jnp.int32),
        ),
        grid=(groups,),
        in_specs=[
            pl.BlockSpec(memory_space=pltpu.SMEM),
            pl.BlockSpec(memory_space=pltpu.SMEM),
            pl.BlockSpec((1, PROBES, sounds), lambda g: (g, 0, 0)),
            pl.BlockSpec((groups, sounds), lambda g: (0, 0)),
            pl.BlockSpec((1, slots, sounds, span), lambda g: (g, 0, 0, 0)),
        ],
        out_specs=(
            pl.BlockSpec((128, 2 * SLOT_ROWS, CELLS), lambda g: (0, 0, 0)),
            pl.BlockSpec(memory_space=pltpu.SMEM),
            pl.BlockSpec(memory_space=pltpu.SMEM),
        ),
        scratch_shapes=[pltpu.SMEM((128,), jnp.int32)],
        compiler_params=pltpu.CompilerParams(vmem_limit_bytes=24 * MIB),
        name="adjoint",
    )(grid_tile, counts, probes, precision, footprints)


def receive_kernel(idx_ref, arr_ref, scale_ref, hi_ref, lo_ref, acc_a, acc_b):
    zero = jnp.zeros((SLOT_ROWS, CELLS), jnp.float32)

    def clear(i, carry):
        acc_a[i] = zero
        acc_b[i] = zero
        return carry

    lax.fori_loop(0, TILES, clear, 0, unroll=8)

    def add(d, carry):
        ia = idx_ref[2 * d]
        ib = idx_ref[2 * d + 1]
        acc_a[ia] += arr_ref[d, :SLOT_ROWS, :].astype(jnp.float32)
        acc_b[ib] += arr_ref[d, SLOT_ROWS:, :].astype(jnp.float32)
        return carry

    lax.fori_loop(0, 128, add, 0, unroll=4)

    for tc in range(ACROSS):

        def finish(tr, carry):
            t = tc * DOWN + tr
            x = [acc_a[t, w * 8 : w * 8 + 8, :] + acc_b[t, w * 8 : w * 8 + 8, :] for w in range(WEEKS)]
            scale = scale_ref[tc, pl.ds(tr, 1), :]
            ahead = [x[0]]
            for w in range(1, WEEKS):
                ahead.append(x[w] + week_decay * ahead[-1])
            mixed = [None] * WEEKS
            mixed[WEEKS - 1] = ahead[WEEKS - 1]
            behind = week_decay * x[WEEKS - 1]
            for w in range(WEEKS - 2, -1, -1):
                mixed[w] = ahead[w] + behind
                behind = week_decay * (x[w] + behind)
            y = jnp.concatenate(mixed, axis=0) * scale
            hi = y.astype(jnp.bfloat16)
            hi_ref[tc, tr] = hi
            lo_ref[tc, tr] = (y - hi.astype(jnp.float32)).astype(jnp.bfloat16)
            return carry

        lax.fori_loop(0, DOWN, finish, 0, unroll=4)


def receive_call(index, arrived, scale):
    shape = jax.ShapeDtypeStruct((ACROSS, DOWN, SLOT_ROWS, CELLS), jnp.bfloat16)
    return pl.pallas_call(
        receive_kernel,
        out_shape=(shape, shape),
        in_specs=[
            pl.BlockSpec(memory_space=pltpu.SMEM),
            pl.BlockSpec(memory_space=pltpu.VMEM),
            pl.BlockSpec(memory_space=pltpu.VMEM),
        ],
        out_specs=(pl.BlockSpec(memory_space=pltpu.VMEM),) * 2,
        scratch_shapes=[
            pltpu.VMEM((TILES + 1, SLOT_ROWS, CELLS), jnp.float32),
            pltpu.VMEM((TILES + 1, SLOT_ROWS, CELLS), jnp.float32),
        ],
        compiler_params=pltpu.CompilerParams(vmem_limit_bytes=24 * MIB),
        name="receive",
    )(index, arrived, scale)


def diffuse_kernel(
    where_ref, idx_ref, hi_ref, lo_ref, north_ref, south_ref, west_ref, east_ref, scale_ref, weight_ref, mirror_ref,
    inc_ref, reply_ref, half_ref, nh, sh, wh, eh, left_ref,
):
    lat, lon = where_ref[0], where_ref[1]
    flat = (SLOT_ROWS, CELLS)

    def mirrored(block, side):
        rows = block.reshape(-1, CELLS)
        out = jnp.dot(rows, mirror_ref[side], preferred_element_type=jnp.float32)
        return out.astype(jnp.bfloat16).reshape(block.shape)

    nh[...] = north_ref[...]
    sh[...] = south_ref[...]
    wh[...] = west_ref[...]
    eh[...] = east_ref[...]

    @pl.when(lat == 0)
    def _():
        for tc in range(ACROSS):
            nh[tc] = mirrored(hi_ref[tc, 0], 0)

    @pl.when(lat == 3)
    def _():
        for tc in range(ACROSS):
            sh[tc] = mirrored(hi_ref[tc, DOWN - 1], 1)

    @pl.when(lon == 0)
    def _():
        wh[0] = mirrored(nh[0], 2)
        wh[1 : DOWN + 1] = mirrored(hi_ref[0], 2)
        wh[DOWN + 1] = mirrored(sh[0], 2)

    @pl.when(lon == 31)
    def _():
        eh[0] = mirrored(nh[ACROSS - 1], 3)
        eh[1 : DOWN + 1] = mirrored(hi_ref[ACROSS - 1], 3)
        eh[DOWN + 1] = mirrored(sh[ACROSS - 1], 3)

    @pl.when(lat == 0)
    def _():
        wh[0] = mirrored(wh[1], 0)
        eh[0] = mirrored(eh[1], 0)

    @pl.when(lat == 3)
    def _():
        wh[DOWN + 1] = mirrored(wh[DOWN], 1)
        eh[DOWN + 1] = mirrored(eh[DOWN], 1)

    lane = lax.broadcasted_iota(jnp.int32, flat, 1)
    upper = lane < 64
    east_side = jnp.bitwise_and(lane, 15) < 8
    chunk = 8
    zero = jnp.zeros(flat, jnp.bfloat16)

    for pair in range(ACROSS // 2):
        for part in range(DOWN // chunk):
            total = None
            for ref, is_hi in ((hi_ref, True), (lo_ref, False)):

                def tile(x, tr):
                    if x < 0 or x >= ACROSS:
                        if not is_hi:
                            return zero
                        return (wh if x < 0 else eh)[tr + 1]
                    if tr < 0 or tr >= DOWN:
                        if not is_hi:
                            return zero
                        return (nh if tr < 0 else sh)[x]
                    return ref[x, tr]

                for k in range(chunk):
                    tr = part * chunk + k
                    own, both = [], []
                    for x in range(2 * pair - 1, 2 * pair + 3):
                        own.append(tile(x, tr))
                        both.append(jnp.where(upper, tile(x, tr + 1), tile(x, tr - 1)))
                    rows = slice(k * SLOT_ROWS, (k + 1) * SLOT_ROWS)
                    left_ref[rows, 0:128] = own[1]
                    left_ref[rows, 128:256] = own[2]
                    left_ref[rows, 256:384] = jnp.where(east_side, own[3], own[0])
                    left_ref[rows, 384:512] = both[1]
                    left_ref[rows, 512:640] = both[2]
                    left_ref[rows, 640:768] = jnp.where(east_side, both[3], both[0])
                product = jnp.dot(left_ref[...], weight_ref[...], preferred_element_type=jnp.float32)
                total = product if total is None else total + product
            for k in range(chunk):
                tr = part * chunk + k
                for u in range(2):
                    tc = 2 * pair + u
                    scale = scale_ref[tc, tr : tr + 1, :] * STEP_FACTOR
                    y = total[k * SLOT_ROWS : (k + 1) * SLOT_ROWS, u * 128 : (u + 1) * 128] * scale
                    inc_ref[tc, tr] = y
                    half_ref[tc * DOWN + tr] = y.astype(jnp.bfloat16)

    def answer(d, carry):
        reply_ref[d, :SLOT_ROWS, :] = half_ref[idx_ref[2 * d]]
        reply_ref[d, SLOT_ROWS:, :] = half_ref[idx_ref[2 * d + 1]]
        return carry

    lax.fori_loop(0, 128, answer, 0, unroll=8)


def diffuse_call(where, index, hi, lo, north, south, west, east, scale, weight, mirror):
    vmem = pl.BlockSpec(memory_space=pltpu.VMEM)
    smem = pl.BlockSpec(memory_space=pltpu.SMEM)
    return pl.pallas_call(
        diffuse_kernel,
        out_shape=(
            jax.ShapeDtypeStruct((ACROSS, DOWN, SLOT_ROWS, CELLS), jnp.float32),
            jax.ShapeDtypeStruct((128, 2 * SLOT_ROWS, CELLS), jnp.bfloat16),
        ),
        in_specs=[smem, smem] + [vmem] * 9,
        out_specs=(vmem, vmem),
        scratch_shapes=[
            pltpu.VMEM((TILES + 1, SLOT_ROWS, CELLS), jnp.bfloat16),
            pltpu.VMEM((ACROSS, SLOT_ROWS, CELLS), jnp.bfloat16),
            pltpu.VMEM((ACROSS, SLOT_ROWS, CELLS), jnp.bfloat16),
            pltpu.VMEM((DOWN + 2, SLOT_ROWS, CELLS), jnp.bfloat16),
            pltpu.VMEM((DOWN + 2, SLOT_ROWS, CELLS), jnp.bfloat16),
            pltpu.VMEM((8 * SLOT_ROWS, 768), jnp.bfloat16),
        ],
        compiler_params=pltpu.CompilerParams(vmem_limit_bytes=32 * MIB),
        name="diffuse",
    )(where, index, hi, lo, north, south, west, east, scale, weight, mirror)


def layout_kernel(inc_ref, out_ref, rows_ref):
    lane = lax.broadcasted_iota(jnp.int32, (8, CELLS), 1)
    group = lax.shift_right_logical(lane, 4)

    def regroup(tr, carry):
        for half in range(2):
            v = [
                inc_ref[i % 4, tr, (half * 2 + i // 4) * 8 : (half * 2 + i // 4) * 8 + 8, :] for i in range(8)
            ]
            for bit in (1, 2, 4):
                clear = jnp.bitwise_and(group, bit) == 0
                for i in range(8):
                    if i & bit == 0:
                        a, c = v[i], v[i + bit]
                        v[i] = jnp.where(clear, a, pltpu.roll(c, 16 * bit, 1))
                        v[i + bit] = jnp.where(clear, pltpu.roll(a, 128 - 16 * bit, 1), c)
            for r in range(8):
                at = pl.multiple_of((half * 256 + tr * 8 + r) * 8, 8)
                rows_ref[pl.ds(at, 8), :] = v[r]
        return carry

    lax.fori_loop(0, DOWN, regroup, 0, unroll=2)

    for half in range(2):
        for p in range(PROBES):
            for k in range(2):
                block = rows_ref[pl.ds((half * 256 + k * 128) * 8 + p, 128, stride=8), :]
                out_ref[pl.ds((p * 4 + half * 2) * 64, 128), k * 128 : (k + 1) * 128] = block.T


def layout_call(inc):
    return pl.pallas_call(
        layout_kernel,
        out_shape=jax.ShapeDtypeStruct((SLOT_ROWS * 64, 256), jnp.float32),
        in_specs=[pl.BlockSpec(memory_space=pltpu.VMEM)],
        out_specs=pl.BlockSpec(memory_space=pltpu.VMEM),
        scratch_shapes=[pltpu.VMEM((2 * 256 * 8, CELLS), jnp.float32)],
        compiler_params=pltpu.CompilerParams(vmem_limit_bytes=16 * MIB),
        cost_estimate=pl.CostEstimate(flops=8 * MIB, bytes_accessed=8 * MIB, transcendentals=0),
        name="layout",
    )(inc)


def forward_kernel(pos_ref, count_ref, tiles_ref, foot_ref, out_ref):
    g = pl.program_id(0)
    slots = foot_ref.shape[1]
    count = count_ref[g]
    total = jnp.zeros((PROBES, foot_ref.shape[2]), jnp.float32)
    for j in range(slots):
        place = pos_ref[g * slots + j]
        at = pl.multiple_of(jnp.bitwise_and(place, 1) * SLOT_ROWS, SLOT_ROWS)
        tile = tiles_ref[lax.shift_right_logical(place, 1), pl.ds(at, SLOT_ROWS), :].astype(jnp.float32)
        left = jnp.concatenate([tile[w * 8 : w * 8 + 8] for w in range(WEEKS)], axis=1).astype(jnp.bfloat16)
        value = lax.dot_general(
            left, foot_ref[0, j], (((1,), (1,)), ((), ())), preferred_element_type=jnp.float32
        )
        total = total + (value if j < 6 else jnp.where(j < count, value, 0.0))
    out_ref[0] = total


def forward_call(pos, counts, tiles, footprints):
    groups, slots, sounds, span = footprints.shape
    return pl.pallas_call(
        forward_kernel,
        out_shape=jax.ShapeDtypeStruct((groups, PROBES, sounds), jnp.float32),
        grid=(groups,),
        in_specs=[
            pl.BlockSpec(memory_space=pltpu.SMEM),
            pl.BlockSpec(memory_space=pltpu.SMEM),
            pl.BlockSpec((128, 2 * SLOT_ROWS, CELLS), lambda g: (0, 0, 0)),
            pl.BlockSpec((1, slots, sounds, span), lambda g: (g, 0, 0, 0)),
        ],
        out_specs=pl.BlockSpec((1, PROBES, sounds), lambda g: (g, 0, 0)),
        compiler_params=pltpu.CompilerParams(vmem_limit_bytes=24 * MIB),
        name="forward",
    )(pos, counts, tiles, footprints)


def exchanged(block):
    return lax.all_to_all(block, ("lat", "lon"), split_axis=0, concat_axis=0, tiled=True)


def per_device(
    footprints, tile_lists, tile_counts, tile_place, probes, obs_precision, prior_sigma, land_mask
):
    lat, lon = lax.axis_index("lat"), lax.axis_index("lon")
    me = lat * 32 + lon
    grid_tile = tile_place[tile_lists.reshape(-1)]
    outgoing, table, pos = adjoint_call(grid_tile, tile_counts, probes, obs_precision, footprints)
    arrived = exchanged(outgoing)
    tables = lax.all_gather(table, ("lat", "lon"), axis=0, tiled=False)
    index = lax.dynamic_slice(tables, (0, 2 * me), (128, 2)).reshape(256)

    scale = prior_sigma * land_mask.astype(jnp.float32)
    scale = scale.reshape(DOWN, TILE_ROWS, ACROSS, TILE_COLS).transpose(2, 0, 1, 3).reshape(ACROSS, DOWN, CELLS)

    hi, lo = receive_call(index, arrived, scale)

    south_way = [(i, i + 1) for i in range(3)]
    north_way = [(i + 1, i) for i in range(3)]
    east_way = [(i, i + 1) for i in range(31)]
    west_way = [(i + 1, i) for i in range(31)]
    north = lax.ppermute(hi[:, DOWN - 1], "lat", south_way)
    south = lax.ppermute(hi[:, 0], "lat", north_way)
    edge_w = jnp.concatenate([north[:1], hi[0], south[:1]], axis=0)
    edge_e = jnp.concatenate([north[3:], hi[ACROSS - 1], south[3:]], axis=0)
    west = lax.ppermute(edge_e, "lon", east_way)
    east = lax.ppermute(edge_w, "lon", west_way)

    where = jnp.stack([lat, lon]).astype(jnp.int32)
    weight = jnp.asarray(stencil_weights(), jnp.bfloat16)
    mirror = jnp.asarray(reflections(), jnp.bfloat16)
    inc, reply = diffuse_call(where, index, hi, lo, north, south, west, east, scale, weight, mirror)
    returned = exchanged(reply)
    increment = layout_call(inc).reshape(SLOT_ROWS, 64, 256).transpose(2, 0, 1)
    predicted = forward_call(pos, tile_counts, returned, footprints)
    return (predicted, increment)


def solution(mesh):
    in_specs = (
        P(("lat", "lon"), None, None, None),
        P(("lat", "lon"), None),
        P(("lat", "lon")),
        P(),
        P(("lat", "lon"), None, None),
        P(("lat", "lon"), None),
        P("lat", "lon"),
        P("lat", "lon"),
    )
    out_specs = (P(("lat", "lon"), None, None), P("lat", None, "lon"))
    return jax.shard_map(
        per_device, mesh=mesh, in_specs=in_specs, out_specs=out_specs, check_vma=False
    )
```

```python
import functools

import jax
import jax.numpy as jnp
import numpy as np
from jax import lax
from jax.experimental import pallas as pl
from jax.experimental.pallas import tpu as pltpu
from jax.sharding import PartitionSpec as P

TILE_ROWS = 8
TILE_COLS = 16
WEEKS = 4
PROBES = 8
NSTEP = 4
CELLS = 128
SLOT_ROWS = WEEKS * PROBES
DOWN = 32
ACROSS = 4
TILES = DOWN * ACROSS
SEND_ROWS = 2 * SLOT_ROWS + 8
QUADS = DOWN // 4

diffusion_rate = 0.2
week_decay = 0.6
MIB = 1 << 20

STEP_FACTOR = diffusion_rate**NSTEP


def stencil_coefficients():
    out = np.zeros((9, 9), np.int64)
    out[4, 4] = 1
    for _ in range(NSTEP):
        padded = np.pad(out, 1)
        out = (
            padded[1:-1, 1:-1]
            + padded[2:, 1:-1]
            + padded[:-2, 1:-1]
            + padded[1:-1, 2:]
            + padded[1:-1, :-2]
        )
    return out


def stencil_weights():
    coef = stencil_coefficients()
    lane = np.arange(128)
    r, c = lane // 16, lane % 16
    rows_own = r
    rows_ns = np.where(r < 4, 8 + r, r - 8)
    cols_ew = np.where(c < 8, 32 + c, c - 16)
    row_in = np.concatenate([rows_own] * 3 + [rows_ns] * 3)
    col_in = np.concatenate([c, 16 + c, cols_ew] * 2)
    row_out = np.concatenate([r, r])
    col_out = np.concatenate([c, 16 + c])
    dr = row_in[:, None] - row_out[None, :]
    dc = col_in[:, None] - col_out[None, :]
    near = (np.abs(dr) <= 4) & (np.abs(dc) <= 4)
    return np.where(near, coef[np.clip(dr + 4, 0, 8), np.clip(dc + 4, 0, 8)], 0).astype(np.float32)


def reflections():
    out = np.zeros((4, 128, 128), np.float32)
    for k in range(1, 4):
        for c in range(16):
            out[0, (k - 1) * 16 + c, (7 - k) * 16 + c] = -1
            out[1, (8 - k) * 16 + c, k * 16 + c] = -1
        for r in range(8):
            out[2, r * 16 + k - 1, r * 16 + 15 - k] = -1
            out[3, r * 16 + 16 - k, r * 16 + k] = -1
    return out


def in_hbm(x):
    return pltpu.with_memory_space_constraint(x, pltpu.HBM)


def adjoint_kernel(
    list_hbm, count_hbm, place_hbm, probe_hbm, prec_hbm, foot_hbm, out_hbm, pos_ref,
    foot, packed, probe_ref, prec_ref, list_ref, count_ref, place_ref, table_ref, seen_ref, small_sem, foot_sem, out_sem,
):
    groups, slots = foot.shape[:2]
    pairs = slots // 2
    small = [
        pltpu.make_async_copy(src, dst, small_sem.at[k])
        for k, (src, dst) in enumerate(
            (
                (count_hbm, count_ref),
                (list_hbm, list_ref),
                (place_hbm, place_ref),
                (probe_hbm, probe_ref),
                (prec_hbm, prec_ref),
            )
        )
    ]
    for copy in small:
        copy.start()

    def fetch(g, j):
        return pltpu.make_async_copy(foot_hbm.at[g, pl.ds(2 * j, 2)], foot.at[g, pl.ds(2 * j, 2)], foot_sem.at[g, j])

    def start_sure(g, carry):
        for j in range(3):
            fetch(g, j).start()
        return carry

    def start_rest(g, carry):
        count = count_ref[g]
        for j in range(3, pairs):

            @pl.when(2 * j < count)
            def _():
                fetch(g, j).start()

        return carry

    start_sure(0, 0)
    small[0].wait()
    start_rest(0, 0)

    def start_group(g, carry):
        start_sure(g, carry)
        return start_rest(g, carry)

    lax.fori_loop(1, groups, start_group, 0)

    def clear(i, carry):
        table_ref[2 * i] = TILES
        table_ref[2 * i + 1] = TILES
        seen_ref[i] = 0
        return carry

    lax.fori_loop(0, 129, clear, 0, unroll=3)
    for copy in small[1:]:
        copy.wait()

    def group(g, carry):
        count = count_ref[g]
        weighted = prec_ref[pl.ds(g, 1), :] * probe_ref[g]
        zero = jnp.zeros_like(weighted)
        left = jnp.concatenate(
            [jnp.concatenate([weighted, zero], axis=1), jnp.concatenate([zero, weighted], axis=1)], axis=0
        ).astype(jnp.bfloat16)

        def route(j):
            t = place_ref[list_ref[g, j]]
            row = lax.shift_right_logical(t, 7)
            col = jnp.bitwise_and(t, 127)
            owner = lax.shift_right_logical(row, 5) * 32 + lax.shift_right_logical(col, 2)
            local = jnp.bitwise_and(col, 3) * DOWN + jnp.bitwise_and(row, 31)
            live = j < count
            owner = jnp.where(live, owner, 128)
            rank = jnp.minimum(seen_ref[owner], 1)
            seen_ref[owner] = rank + 1
            place = owner * 2 + rank
            table_ref[place] = local
            pos_ref[g * slots + j] = jnp.where(live, place, -1)
            return owner, rank

        def pair(j):
            both = jnp.dot(left, foot[g, 2 * j : 2 * j + 2].reshape(256, -1), preferred_element_type=jnp.float32)
            for u in range(2):
                owner, rank = route(2 * j + u)
                part = both[u * 8 : u * 8 + 8]
                part = jnp.concatenate([part[:, w * CELLS : (w + 1) * CELLS] for w in range(WEEKS)], axis=0)
                at = pl.multiple_of(rank * SLOT_ROWS, SLOT_ROWS)
                packed[owner, pl.ds(at, SLOT_ROWS), :] = part.astype(jnp.bfloat16)

        for n in range(3, pairs + 1):

            @pl.when((count + 1) // 2 == n)
            def _():
                for j in range(n):
                    fetch(g, j).wait()
                for j in range(n):
                    pair(j)
                for j in range(2 * n, slots):
                    pos_ref[g * slots + j] = -1

        return carry

    lax.fori_loop(0, groups, group, 0)

    first = lax.broadcasted_iota(jnp.int32, (8, CELLS), 0) < 4

    def note(d, carry):
        value = jnp.where(first, table_ref[2 * d], table_ref[2 * d + 1])
        packed[d, 64:72, :] = value.astype(jnp.float32).astype(jnp.bfloat16)
        return carry

    copies = []
    for k in range(4):
        lax.fori_loop(32 * k, 32 * k + 32, note, 0, unroll=8)
        part = pl.ds(32 * k, 32)
        copies.append(pltpu.make_async_copy(packed.at[part], out_hbm.at[part], out_sem.at[k]))
        copies[-1].start()
    for copy in copies:
        copy.wait()


def adjoint_call(tile_lists, counts, tile_place, probes, precision, footprints):
    groups, slots, sounds, span = footprints.shape
    smem = pl.BlockSpec(memory_space=pltpu.SMEM)
    hbm = pl.BlockSpec(memory_space=pltpu.HBM)
    return pl.pallas_call(
        adjoint_kernel,
        out_shape=(
            pltpu.HBM((128, SEND_ROWS, CELLS), jnp.bfloat16),
            jax.ShapeDtypeStruct((groups * slots,), jnp.int32),
        ),
        in_specs=[hbm] * 6,
        out_specs=(hbm, smem),
        scratch_shapes=[
            pltpu.VMEM((groups, slots, sounds, span), jnp.bfloat16),
            pltpu.VMEM((129, SEND_ROWS, CELLS), jnp.bfloat16),
            pltpu.VMEM(probes.shape, probes.dtype),
            pltpu.VMEM(precision.shape, precision.dtype),
            pltpu.SMEM(tile_lists.shape, jnp.int32),
            pltpu.SMEM(counts.shape, jnp.int32),
            pltpu.SMEM(tile_place.shape, jnp.int32),
            pltpu.SMEM((258,), jnp.int32),
            pltpu.SMEM((129,), jnp.int32),
            pltpu.SemaphoreType.DMA((5,)),
            pltpu.SemaphoreType.DMA((groups, slots // 2)),
            pltpu.SemaphoreType.DMA((4,)),
        ],
        compiler_params=pltpu.CompilerParams(vmem_limit_bytes=32 * MIB),
        name="adjoint",
    )(*map(in_hbm, (tile_lists, counts, tile_place, probes, precision, footprints)))


def receive_kernel(
    where_ref, arr_ref, scale_ref, hi_ref, lo_hbm, first_ref, second_ref, west_ref, east_ref, idx_ref,
    acc_a, acc_b, lo_ref, idx_vec, idx_sem, out_sem,
):
    zero = jnp.zeros((SLOT_ROWS, CELLS), jnp.float32)
    lane8 = lax.broadcasted_iota(jnp.int32, (8, CELLS), 1)

    def gather(d, found):
        return jnp.where(lane8 == d, arr_ref[d, 64:72, :].astype(jnp.float32), found)

    found = lax.fori_loop(0, 128, gather, jnp.zeros((8, CELLS), jnp.float32), unroll=8)
    idx_vec[...] = found.astype(jnp.int32)
    idx_copy = pltpu.make_async_copy(idx_vec, idx_ref, idx_sem)
    idx_copy.start()

    def clear(i, carry):
        acc_a[i] = zero
        acc_b[i] = zero
        return carry

    lax.fori_loop(0, TILES, clear, 0, unroll=8)
    idx_copy.wait()

    def add(d, carry):
        ia = idx_ref[0, d]
        ib = idx_ref[4, d]
        acc_a[ia] += arr_ref[d, :SLOT_ROWS, :].astype(jnp.float32)
        acc_b[ib] += arr_ref[d, SLOT_ROWS : 2 * SLOT_ROWS, :].astype(jnp.float32)
        return carry

    lax.fori_loop(0, 128, add, 0, unroll=4)

    lane = lax.broadcasted_iota(jnp.int32, (SLOT_ROWS, CELLS), 1)
    place = lax.shift_right_logical(jnp.bitwise_and(lane, 15), 2)

    copies = []
    even = jnp.bitwise_and(where_ref[0], 1) == 0
    for tc in (1, 2, 0, 3):

        def finish(quad, carry):
            edge = zero
            for k in range(4):
                tr = quad * 4 + k
                t = tc * DOWN + tr
                x = [acc_a[t, w * 8 : w * 8 + 8, :] + acc_b[t, w * 8 : w * 8 + 8, :] for w in range(WEEKS)]
                scale = scale_ref[tc, pl.ds(tr, 1), :]
                ahead = [x[0]]
                for w in range(1, WEEKS):
                    ahead.append(x[w] + week_decay * ahead[-1])
                mixed = [None] * WEEKS
                mixed[WEEKS - 1] = ahead[WEEKS - 1]
                behind = week_decay * x[WEEKS - 1]
                for w in range(WEEKS - 2, -1, -1):
                    mixed[w] = ahead[w] + behind
                    behind = week_decay * (x[w] + behind)
                y = jnp.concatenate(mixed, axis=0) * scale
                hi = y.astype(jnp.bfloat16)
                hi_ref[tc, tr] = hi
                lo_ref[tc, tr] = (y - hi.astype(jnp.float32)).astype(jnp.bfloat16)
                if tc == 0:
                    edge = jnp.where(place == k, pltpu.roll(y, 4 * k, 1), edge)
                if tc == ACROSS - 1:
                    edge = jnp.where(place == k, pltpu.roll(y, (4 * k - 12) % 128, 1), edge)
            if tc == 0:
                west_ref[quad] = edge.astype(jnp.bfloat16)
            if tc == ACROSS - 1:
                east_ref[quad] = edge.astype(jnp.bfloat16)
            return carry

        lax.fori_loop(0, QUADS, finish, 0)
        top = hi_ref[tc, 0]
        bottom = hi_ref[tc, DOWN - 1]
        first_ref[tc] = jnp.where(even, bottom, top)
        second_ref[tc] = jnp.where(even, top, bottom)
        copies.append(pltpu.make_async_copy(lo_ref.at[tc], lo_hbm.at[tc], out_sem.at[tc]))
        copies[-1].start()
    for copy in copies:
        copy.wait()


def receive_call(where, arrived, scale):
    vmem = pl.BlockSpec(memory_space=pltpu.VMEM)
    hbm = pl.BlockSpec(memory_space=pltpu.HBM)
    smem = pl.BlockSpec(memory_space=pltpu.SMEM)
    block = (ACROSS, DOWN, SLOT_ROWS, CELLS)
    row = jax.ShapeDtypeStruct((ACROSS, SLOT_ROWS, CELLS), jnp.bfloat16)
    column = jax.ShapeDtypeStruct((QUADS, SLOT_ROWS, CELLS), jnp.bfloat16)
    return pl.pallas_call(
        receive_kernel,
        out_shape=(
            jax.ShapeDtypeStruct(block, jnp.bfloat16),
            pltpu.HBM(block, jnp.bfloat16),
            row,
            row,
            column,
            column,
            jax.ShapeDtypeStruct((8, 128), jnp.int32),
        ),
        in_specs=[smem, vmem, vmem],
        out_specs=(vmem, hbm) + (vmem,) * 4 + (smem,),
        scratch_shapes=[
            pltpu.VMEM((TILES + 1, SLOT_ROWS, CELLS), jnp.float32),
            pltpu.VMEM((TILES + 1, SLOT_ROWS, CELLS), jnp.float32),
            pltpu.VMEM(block, jnp.bfloat16),
            pltpu.VMEM((8, 128), jnp.int32),
            pltpu.SemaphoreType.DMA,
            pltpu.SemaphoreType.DMA((ACROSS,)),
        ],
        compiler_params=pltpu.CompilerParams(vmem_limit_bytes=24 * MIB),
        name="receive",
    )(where, arrived, scale)


def facing(flag, first, second):
    even = jnp.bitwise_and(flag, 1) == 0
    return jnp.where(even, first, second), jnp.where(even, second, first)


def corner_kernel(where_ref, first_ref, second_ref, west_ref, east_ref, first_out, second_out):
    lane = lax.broadcasted_iota(jnp.int32, (SLOT_ROWS, CELLS), 1)
    place = lax.shift_right_logical(jnp.bitwise_and(lane, 15), 2)
    even = jnp.bitwise_and(where_ref[1], 1) == 0

    def put(quad, west, east):
        first_out[quad] = jnp.where(even, east, west)
        second_out[quad] = jnp.where(even, west, east)

    for quad in range(QUADS):
        put(quad, west_ref[quad], east_ref[quad])
    corners = []
    for tc, shift in ((0, 0), (ACROSS - 1, 116)):
        below, above = facing(
            where_ref[0], first_ref[tc].astype(jnp.float32), second_ref[tc].astype(jnp.float32)
        )
        if shift:
            above = pltpu.roll(above, shift, 1)
        below = pltpu.roll(below, (shift + 4) % 128, 1)
        corners.append(jnp.where(place == 0, above, below).astype(jnp.bfloat16))
    put(QUADS, *corners)


def corner_call(where, first, second, west, east):
    vmem = pl.BlockSpec(memory_space=pltpu.VMEM)
    column = jax.ShapeDtypeStruct((QUADS + 1, SLOT_ROWS, CELLS), jnp.bfloat16)
    return pl.pallas_call(
        corner_kernel,
        out_shape=(column, column),
        in_specs=[pl.BlockSpec(memory_space=pltpu.SMEM)] + [vmem] * 4,
        out_specs=(vmem, vmem),
        compiler_params=pltpu.CompilerParams(vmem_limit_bytes=16 * MIB),
        name="corner",
    )(where, first, second, west, east)


def diffuse_kernel(
    where_ref, idx_ref, hi_ref, lo_hbm, lat_first, lat_second, lon_first, lon_second, scale_ref, weight_hbm, mirror_hbm,
    inc_ref, reply_hbm,
    lo_ref, half_ref, nh, sh, wh, eh, left_ref, reply_ref, weight_ref, mirror_ref, reply_sem, const_sem, field_sem,
):
    lat, lon = where_ref[0], where_ref[1]
    flat = (SLOT_ROWS, CELLS)

    def mirrored(block, side):
        rows = block.reshape(-1, CELLS)
        out = jnp.dot(rows, mirror_ref[side], preferred_element_type=jnp.float32)
        return out.astype(jnp.bfloat16).reshape(block.shape)

    fields = [pltpu.make_async_copy(lo_hbm.at[tc], lo_ref.at[tc], field_sem.at[tc]) for tc in range(ACROSS)]
    for copy in fields:
        copy.start()
    mirror_copy = pltpu.make_async_copy(mirror_hbm, mirror_ref, const_sem.at[0])
    mirror_copy.start()
    weight_copy = pltpu.make_async_copy(weight_hbm, weight_ref, const_sem.at[1])
    weight_copy.start()
    for tc in range(ACROSS):
        sh[tc], nh[tc] = facing(lat, lat_first[tc], lat_second[tc])

    def unpack(i, quad, k):
        east, west = facing(lon, lon_first[quad].astype(jnp.float32), lon_second[quad].astype(jnp.float32))
        wh[i] = pltpu.roll(west, 12 - 4 * k, 1).astype(jnp.bfloat16)
        eh[i] = (pltpu.roll(east, 128 - 4 * k, 1) if k else east).astype(jnp.bfloat16)

    def unpack_quad(quad, carry):
        for k in range(4):
            unpack(quad * 4 + k + 1, quad, k)
        return carry

    lax.fori_loop(0, QUADS, unpack_quad, 0)
    unpack(0, QUADS, 0)
    unpack(DOWN + 1, QUADS, 1)
    mirror_copy.wait()

    @pl.when(lat == 0)
    def _():
        for tc in range(ACROSS):
            nh[tc] = mirrored(hi_ref[tc, 0], 0)

    @pl.when(lat == 3)
    def _():
        for tc in range(ACROSS):
            sh[tc] = mirrored(hi_ref[tc, DOWN - 1], 1)

    @pl.when(lon == 0)
    def _():
        wh[0] = mirrored(nh[0], 2)
        wh[1 : DOWN + 1] = mirrored(hi_ref[0], 2)
        wh[DOWN + 1] = mirrored(sh[0], 2)

    @pl.when(lon == 31)
    def _():
        eh[0] = mirrored(nh[ACROSS - 1], 3)
        eh[1 : DOWN + 1] = mirrored(hi_ref[ACROSS - 1], 3)
        eh[DOWN + 1] = mirrored(sh[ACROSS - 1], 3)

    @pl.when(lat == 0)
    def _():
        wh[0] = mirrored(wh[1], 0)
        eh[0] = mirrored(eh[1], 0)

    @pl.when(lat == 3)
    def _():
        wh[DOWN + 1] = mirrored(wh[DOWN], 1)
        eh[DOWN + 1] = mirrored(eh[DOWN], 1)

    lane = lax.broadcasted_iota(jnp.int32, flat, 1)
    upper = lane < 64
    east_side = jnp.bitwise_and(lane, 15) < 8
    chunk = 8
    zero = jnp.zeros(flat, jnp.bfloat16)
    weight_copy.wait()

    for pair in range(ACROSS // 2):
        for part in range(DOWN // chunk):
            total = None
            for ref, is_hi in ((hi_ref, True), (lo_ref, False)):
                if pair == 0 and part == 0 and not is_hi:
                    for copy in fields:
                        copy.wait()

                def tile(x, tr):
                    if x < 0 or x >= ACROSS:
                        if not is_hi:
                            return zero
                        return (wh if x < 0 else eh)[tr + 1]
                    if tr < 0 or tr >= DOWN:
                        if not is_hi:
                            return zero
                        return (nh if tr < 0 else sh)[x]
                    return ref[x, tr]

                for k in range(chunk):
                    tr = part * chunk + k
                    own, both = [], []
                    for x in range(2 * pair - 1, 2 * pair + 3):
                        own.append(tile(x, tr))
                        both.append(jnp.where(upper, tile(x, tr + 1), tile(x, tr - 1)))
                    rows = slice(k * SLOT_ROWS, (k + 1) * SLOT_ROWS)
                    left_ref[rows, 0:128] = own[1]
                    left_ref[rows, 128:256] = own[2]
                    left_ref[rows, 256:384] = jnp.where(east_side, own[3], own[0])
                    left_ref[rows, 384:512] = both[1]
                    left_ref[rows, 512:640] = both[2]
                    left_ref[rows, 640:768] = jnp.where(east_side, both[3], both[0])
                product = jnp.dot(left_ref[...], weight_ref[...], preferred_element_type=jnp.float32)
                total = product if total is None else total + product
            for k in range(chunk):
                tr = part * chunk + k
                for u in range(2):
                    tc = 2 * pair + u
                    scale = scale_ref[tc, tr : tr + 1, :] * STEP_FACTOR
                    y = total[k * SLOT_ROWS : (k + 1) * SLOT_ROWS, u * 128 : (u + 1) * 128] * scale
                    inc_ref[tc, tr] = y
                    half_ref[tc * DOWN + tr] = y.astype(jnp.bfloat16)

    def answer(d, carry):
        reply_ref[d, :SLOT_ROWS, :] = half_ref[idx_ref[0, d]]
        reply_ref[d, SLOT_ROWS:, :] = half_ref[idx_ref[4, d]]
        return carry

    copies = []
    for k in range(4):
        lax.fori_loop(32 * k, 32 * k + 32, answer, 0, unroll=8)
        part = pl.ds(32 * k, 32)
        copies.append(pltpu.make_async_copy(reply_ref.at[part], reply_hbm.at[part], reply_sem.at[k]))
        copies[-1].start()
    for copy in copies:
        copy.wait()


def diffuse_call(where, index, hi, lo, halos, scale, weight, mirror):
    vmem = pl.BlockSpec(memory_space=pltpu.VMEM)
    smem = pl.BlockSpec(memory_space=pltpu.SMEM)
    hbm = pl.BlockSpec(memory_space=pltpu.HBM)
    return pl.pallas_call(
        diffuse_kernel,
        out_shape=(
            jax.ShapeDtypeStruct((ACROSS, DOWN, SLOT_ROWS, CELLS), jnp.float32),
            pltpu.HBM((128, 2 * SLOT_ROWS, CELLS), jnp.bfloat16),
        ),
        in_specs=[smem, smem, vmem, hbm] + [vmem] * 5 + [hbm] * 2,
        out_specs=(vmem, hbm),
        scratch_shapes=[
            pltpu.VMEM((ACROSS, DOWN, SLOT_ROWS, CELLS), jnp.bfloat16),
            pltpu.VMEM((TILES + 1, SLOT_ROWS, CELLS), jnp.bfloat16),
            pltpu.VMEM((ACROSS, SLOT_ROWS, CELLS), jnp.bfloat16),
            pltpu.VMEM((ACROSS, SLOT_ROWS, CELLS), jnp.bfloat16),
            pltpu.VMEM((DOWN + 2, SLOT_ROWS, CELLS), jnp.bfloat16),
            pltpu.VMEM((DOWN + 2, SLOT_ROWS, CELLS), jnp.bfloat16),
            pltpu.VMEM((8 * SLOT_ROWS, 768), jnp.bfloat16),
            pltpu.VMEM((128, 2 * SLOT_ROWS, CELLS), jnp.bfloat16),
            pltpu.VMEM(weight.shape, weight.dtype),
            pltpu.VMEM(mirror.shape, mirror.dtype),
            pltpu.SemaphoreType.DMA((4,)),
            pltpu.SemaphoreType.DMA((2,)),
            pltpu.SemaphoreType.DMA((ACROSS,)),
        ],
        compiler_params=pltpu.CompilerParams(vmem_limit_bytes=32 * MIB),
        name="diffuse",
    )(where, index, hi, in_hbm(lo), *halos, scale, in_hbm(weight), in_hbm(mirror))


def layout_kernel(inc_ref, out_ref, rows_ref):
    lane = lax.broadcasted_iota(jnp.int32, (8, CELLS), 1)
    group = lax.shift_right_logical(lane, 4)

    def regroup(tr, carry):
        for half in range(2):
            v = [
                inc_ref[i % 4, tr, (half * 2 + i // 4) * 8 : (half * 2 + i // 4) * 8 + 8, :] for i in range(8)
            ]
            for bit in (1, 2, 4):
                clear = jnp.bitwise_and(group, bit) == 0
                for i in range(8):
                    if i & bit == 0:
                        a, c = v[i], v[i + bit]
                        v[i] = jnp.where(clear, a, pltpu.roll(c, 16 * bit, 1))
                        v[i + bit] = jnp.where(clear, pltpu.roll(a, 128 - 16 * bit, 1), c)
            for r in range(8):
                at = pl.multiple_of((half * 256 + tr * 8 + r) * 8, 8)
                rows_ref[pl.ds(at, 8), :] = v[r]
        return carry

    lax.fori_loop(0, DOWN, regroup, 0, unroll=2)

    for half in range(2):
        for p in range(PROBES):
            for k in range(2):
                block = rows_ref[pl.ds((half * 256 + k * 128) * 8 + p, 128, stride=8), :]
                out_ref[pl.ds((p * 4 + half * 2) * 64, 128), k * 128 : (k + 1) * 128] = block.T


def layout_call(inc):
    vmem = pl.BlockSpec(memory_space=pltpu.VMEM)
    return pl.pallas_call(
        layout_kernel,
        out_shape=jax.ShapeDtypeStruct((SLOT_ROWS * 64, 256), jnp.float32),
        in_specs=[vmem],
        out_specs=vmem,
        scratch_shapes=[pltpu.VMEM((2 * 256 * 8, CELLS), jnp.float32)],
        compiler_params=pltpu.CompilerParams(vmem_limit_bytes=16 * MIB),
        cost_estimate=pl.CostEstimate(flops=8 * MIB, bytes_accessed=8 * MIB, transcendentals=0),
        name="layout",
    )(inc)


def forward_kernel(pos_ref, tiles_ref, foot_hbm, out_ref, foot, foot_sem):
    groups, slots, sounds, span = foot.shape
    pairs = slots // 2

    def fetch(g, j):
        return pltpu.make_async_copy(foot_hbm.at[g, pl.ds(2 * j, 2)], foot.at[g, pl.ds(2 * j, 2)], foot_sem.at[g, j])

    def start_group(g, carry):
        for j in range(pairs):
            if j < 3:
                fetch(g, j).start()
            else:

                @pl.when(pos_ref[g * slots + 2 * j] >= 0)
                def _():
                    fetch(g, j).start()

        return carry

    lax.fori_loop(0, groups, start_group, 0)

    def group(g, carry):
        def one(j):
            found = pos_ref[g * slots + j]
            place = jnp.maximum(found, 0)
            at = pl.multiple_of(jnp.bitwise_and(place, 1) * SLOT_ROWS, SLOT_ROWS)
            tile = tiles_ref[lax.shift_right_logical(place, 1), pl.ds(at, SLOT_ROWS), :].astype(jnp.float32)
            left = jnp.concatenate([tile[w * 8 : w * 8 + 8] for w in range(WEEKS)], axis=1).astype(jnp.bfloat16)
            value = lax.dot_general(
                left, foot[g, j], (((1,), (1,)), ((), ())), preferred_element_type=jnp.float32
            )
            return value if j < 6 else jnp.where(found >= 0, value, 0.0)

        live = sum((pos_ref[g * slots + 2 * j] >= 0).astype(jnp.int32) for j in range(3, pairs)) + 3
        for n in range(3, pairs + 1):

            @pl.when(live == n)
            def _():
                for j in range(n):
                    fetch(g, j).wait()
                total = one(0)
                for j in range(1, 2 * n):
                    total = total + one(j)
                out_ref[g] = total

        return carry

    lax.fori_loop(0, groups, group, 0)


def forward_call(pos, tiles, footprints):
    groups, slots, sounds, span = footprints.shape
    smem = pl.BlockSpec(memory_space=pltpu.SMEM)
    vmem = pl.BlockSpec(memory_space=pltpu.VMEM)
    return pl.pallas_call(
        forward_kernel,
        out_shape=jax.ShapeDtypeStruct((groups, PROBES, sounds), jnp.float32),
        in_specs=[smem, vmem, pl.BlockSpec(memory_space=pltpu.HBM)],
        out_specs=vmem,
        scratch_shapes=[
            pltpu.VMEM(footprints.shape, footprints.dtype),
            pltpu.SemaphoreType.DMA((groups, slots // 2)),
        ],
        compiler_params=pltpu.CompilerParams(vmem_limit_bytes=32 * MIB),
        name="forward",
    )(pos, tiles, in_hbm(footprints))


def exchanged(block):
    return lax.all_to_all(block, ("lat", "lon"), split_axis=0, concat_axis=0, tiled=True)


def swaps(count, start):
    lower = [(i, i + 1) for i in range(start, count - 1, 2)]
    return lower + [(j, i) for i, j in lower]


def per_device(
    footprints, tile_lists, tile_counts, tile_place, probes, obs_precision, prior_sigma, land_mask
):
    lat, lon = lax.axis_index("lat"), lax.axis_index("lon")
    outgoing, pos = adjoint_call(tile_lists, tile_counts, tile_place, probes, obs_precision, footprints)
    arrived = exchanged(outgoing)

    scale = prior_sigma * land_mask.astype(jnp.float32)
    scale = scale.reshape(DOWN, TILE_ROWS, ACROSS, TILE_COLS).transpose(2, 0, 1, 3).reshape(ACROSS, DOWN, CELLS)

    where = jnp.stack([lat, lon]).astype(jnp.int32)
    hi, lo, lat_one, lat_two, left, right, index = receive_call(where, arrived, scale)
    lat_one = lax.ppermute(lat_one, "lat", swaps(4, 0))
    lat_two = lax.ppermute(lat_two, "lat", swaps(4, 1))
    lon_one, lon_two = corner_call(where, lat_one, lat_two, left, right)
    lon_one = lax.ppermute(lon_one, "lon", swaps(32, 0))
    lon_two = lax.ppermute(lon_two, "lon", swaps(32, 1))
    halos = (lat_one, lat_two, lon_one, lon_two)

    weight = jnp.asarray(stencil_weights(), jnp.bfloat16)
    mirror = jnp.asarray(reflections(), jnp.bfloat16)
    inc, reply = diffuse_call(where, index, hi, lo, halos, scale, weight, mirror)
    returned = exchanged(reply)
    increment = layout_call(inc).reshape(SLOT_ROWS, 64, 256).transpose(2, 0, 1)
    predicted = forward_call(pos, returned, footprints)
    return (predicted, increment)


def solution(mesh):
    in_specs = (
        P(("lat", "lon"), None, None, None),
        P(("lat", "lon"), None),
        P(("lat", "lon")),
        P(),
        P(("lat", "lon"), None, None),
        P(("lat", "lon"), None),
        P("lat", "lon"),
        P("lat", "lon"),
    )
    out_specs = (P(("lat", "lon"), None, None), P("lat", None, "lon"))
    return jax.shard_map(
        per_device, mesh=mesh, in_specs=in_specs, out_specs=out_specs, check_vma=False
    )
```

```python
import functools

import jax
import jax.numpy as jnp
import numpy as np
from jax import lax
from jax.experimental import pallas as pl
from jax.experimental.pallas import tpu as pltpu
from jax.sharding import PartitionSpec as P

TILE_ROWS = 8
TILE_COLS = 16
WEEKS = 4
PROBES = 8
NSTEP = 4
CELLS = 128
SLOT_ROWS = WEEKS * PROBES
DOWN = 32
ACROSS = 4
TILES = DOWN * ACROSS
SEND_ROWS = 2 * SLOT_ROWS + 8
QUADS = DOWN // 4
DIFFUSE_CHUNK = 8
LEAST = 6

diffusion_rate = 0.2
week_decay = 0.6
MIB = 1 << 20

STEP_FACTOR = diffusion_rate**NSTEP


def stencil_coefficients():
    out = np.zeros((9, 9), np.int64)
    out[4, 4] = 1
    for _ in range(NSTEP):
        padded = np.pad(out, 1)
        out = (
            padded[1:-1, 1:-1]
            + padded[2:, 1:-1]
            + padded[:-2, 1:-1]
            + padded[1:-1, 2:]
            + padded[1:-1, :-2]
        )
    return out


def stencil_weights():
    coef = stencil_coefficients()
    lane = np.arange(128)
    r, c = lane // 16, lane % 16
    rows_own = r
    rows_ns = np.where(r < 4, 8 + r, r - 8)
    cols_ew = np.where(c < 8, 32 + c, c - 16)
    row_in = np.concatenate([rows_own] * 3 + [rows_ns] * 3)
    col_in = np.concatenate([c, 16 + c, cols_ew] * 2)
    row_out = np.concatenate([r, r])
    col_out = np.concatenate([c, 16 + c])
    dr = row_in[:, None] - row_out[None, :]
    dc = col_in[:, None] - col_out[None, :]
    near = (np.abs(dr) <= 4) & (np.abs(dc) <= 4)
    return np.where(near, coef[np.clip(dr + 4, 0, 8), np.clip(dc + 4, 0, 8)], 0).astype(np.float32)


def reflections():
    out = np.zeros((4, 128, 128), np.float32)
    for k in range(1, 4):
        for c in range(16):
            out[0, (k - 1) * 16 + c, (7 - k) * 16 + c] = -1
            out[1, (8 - k) * 16 + c, k * 16 + c] = -1
        for r in range(8):
            out[2, r * 16 + k - 1, r * 16 + 15 - k] = -1
            out[3, r * 16 + 16 - k, r * 16 + k] = -1
    return out


def in_hbm(x):
    return pltpu.with_memory_space_constraint(x, pltpu.HBM)


def adjoint_kernel(
    list_hbm, count_hbm, place_hbm, probe_hbm, prec_hbm, foot_hbm, out_hbm, pos_ref,
    foot, packed, probe_ref, prec_ref, list_ref, count_ref, place_ref, seen_ref, small_sem, foot_sem, out_sem,
):
    groups, slots = foot.shape[:2]

    small = [
        pltpu.make_async_copy(src, dst, small_sem.at[k])
        for k, (src, dst) in enumerate(
            (
                (count_hbm, count_ref),
                (list_hbm, list_ref),
                (place_hbm, place_ref),
                (probe_hbm, probe_ref),
                (prec_hbm, prec_ref),
            )
        )
    ]
    for copy in small:
        copy.start()

    def fetch(g, first, last):
        part = (g, pl.ds(first, last - first))
        return pltpu.make_async_copy(foot_hbm.at[part], foot.at[part], foot_sem.at[g, first // LEAST])

    def start_sure(g, carry):
        fetch(g, 0, LEAST).start()
        return carry

    def start_rest(g, carry):
        count = count_ref[g]
        for n in range(LEAST + 1, slots + 1):

            @pl.when(count == n)
            def _():
                fetch(g, LEAST, n).start()

        return carry

    start_sure(0, 0)
    small[0].wait()
    start_rest(0, 0)

    def start_group(g, carry):
        start_sure(g, carry)
        return start_rest(g, carry)

    lax.fori_loop(1, groups, start_group, 0)

    nobody = jnp.full((8, CELLS), TILES, jnp.float32).astype(jnp.bfloat16)
    number_row = lax.shift_right_logical(lax.broadcasted_iota(jnp.int32, (8, CELLS), 0), 2)

    def clear(i, carry):
        seen_ref[i] = 0
        packed[i, 2 * SLOT_ROWS :, :] = nobody
        return carry

    lax.fori_loop(0, 128, clear, 0, unroll=8)
    for copy in small[1:]:
        copy.wait()

    def group(g, carry):
        count = count_ref[g]
        weighted = (prec_ref[pl.ds(g, 1), :] * probe_ref[g]).astype(jnp.bfloat16)

        def route(j):
            t = place_ref[list_ref[g, j]]
            row = lax.shift_right_logical(t, 7)
            col = jnp.bitwise_and(t, 127)
            owner = lax.shift_right_logical(row, 5) * 32 + lax.shift_right_logical(col, 2)
            local = jnp.bitwise_and(col, 3) * DOWN + jnp.bitwise_and(row, 31)
            rank = jnp.minimum(seen_ref[owner], 1)
            seen_ref[owner] = rank + 1
            pos_ref[g * slots + j] = owner * 2 + rank
            return owner, rank, local

        def slot(j):
            part = jnp.dot(weighted, foot[g, j], preferred_element_type=jnp.float32)
            owner, rank, local = route(j)
            part = jnp.concatenate([part[:, w * CELLS : (w + 1) * CELLS] for w in range(WEEKS)], axis=0)
            at = pl.multiple_of(rank * SLOT_ROWS, SLOT_ROWS)
            packed[owner, pl.ds(at, SLOT_ROWS), :] = part.astype(jnp.bfloat16)
            numbers = packed[owner, 2 * SLOT_ROWS :, :].astype(jnp.float32)
            numbers = jnp.where(number_row == rank, local.astype(jnp.float32), numbers)
            packed[owner, 2 * SLOT_ROWS :, :] = numbers.astype(jnp.bfloat16)

        for n in range(LEAST, slots + 1):

            @pl.when(count == n)
            def _():
                fetch(g, 0, LEAST).wait()
                if n > LEAST:
                    fetch(g, LEAST, n).wait()
                for j in range(n):
                    slot(j)
                for j in range(n, slots):
                    pos_ref[g * slots + j] = 0
                pos_ref[groups * slots + g] = n

        return carry

    lax.fori_loop(0, groups, group, 0)

    copies = []
    for k in range(4):
        part = pl.ds(32 * k, 32)
        copies.append(pltpu.make_async_copy(packed.at[part], out_hbm.at[part], out_sem.at[k]))
        copies[-1].start()
    for copy in copies:
        copy.wait()


def adjoint_call(tile_lists, counts, tile_place, probes, precision, footprints):
    groups, slots, sounds, span = footprints.shape
    smem = pl.BlockSpec(memory_space=pltpu.SMEM)
    hbm = pl.BlockSpec(memory_space=pltpu.HBM)
    return pl.pallas_call(
        adjoint_kernel,
        out_shape=(
            pltpu.HBM((128, SEND_ROWS, CELLS), jnp.bfloat16),
            jax.ShapeDtypeStruct((groups * slots + groups,), jnp.int32),
        ),
        in_specs=[hbm] * 6,
        out_specs=(hbm, smem),
        scratch_shapes=[
            pltpu.VMEM((groups, slots, sounds, span), jnp.bfloat16),
            pltpu.VMEM((128, SEND_ROWS, CELLS), jnp.bfloat16),
            pltpu.VMEM(probes.shape, probes.dtype),
            pltpu.VMEM(precision.shape, precision.dtype),
            pltpu.SMEM(tile_lists.shape, jnp.int32),
            pltpu.SMEM(counts.shape, jnp.int32),
            pltpu.SMEM(tile_place.shape, jnp.int32),
            pltpu.SMEM((128,), jnp.int32),
            pltpu.SemaphoreType.DMA((5,)),
            pltpu.SemaphoreType.DMA((groups, 2)),
            pltpu.SemaphoreType.DMA((4,)),
        ],
        compiler_params=pltpu.CompilerParams(vmem_limit_bytes=32 * MIB),
        name="adjoint",
    )(*map(in_hbm, (tile_lists, counts, tile_place, probes, precision, footprints)))


def receive_kernel(
    where_ref, arr_ref, scale_ref, hi_hbm, lo_hbm, first_ref, second_ref, west_ref, east_ref, idx_ref,
    acc_a, acc_b, hi_ref, lo_ref, idx_vec, idx_sem, out_sem,
):
    zero = jnp.zeros((SLOT_ROWS, CELLS), jnp.float32)
    lane8 = lax.broadcasted_iota(jnp.int32, (8, CELLS), 1)

    def gather(d, found):
        return jnp.where(lane8 == d, arr_ref[d, 64:72, :].astype(jnp.float32), found)

    found = lax.fori_loop(0, 128, gather, jnp.zeros((8, CELLS), jnp.float32), unroll=16)
    idx_vec[...] = found.astype(jnp.int32)
    idx_copy = pltpu.make_async_copy(idx_vec, idx_ref, idx_sem)
    idx_copy.start()

    def clear(i, carry):
        acc_a[i] = zero
        acc_b[i] = zero
        return carry

    lax.fori_loop(0, TILES, clear, 0, unroll=8)
    idx_copy.wait()

    def add(d, carry):
        ia = idx_ref[0, d]
        ib = idx_ref[4, d]
        acc_a[ia] += arr_ref[d, :SLOT_ROWS, :].astype(jnp.float32)
        acc_b[ib] += arr_ref[d, SLOT_ROWS : 2 * SLOT_ROWS, :].astype(jnp.float32)
        return carry

    lax.fori_loop(0, 128, add, 0, unroll=8)

    lane = lax.broadcasted_iota(jnp.int32, (SLOT_ROWS, CELLS), 1)
    place = lax.shift_right_logical(jnp.bitwise_and(lane, 15), 2)

    copies = []
    even = jnp.bitwise_and(where_ref[0], 1) == 0
    for tc in (1, 2, 0, 3):

        def finish(quad, carry):
            edge = zero
            for k in range(4):
                tr = quad * 4 + k
                t = tc * DOWN + tr
                x = [acc_a[t, w * 8 : w * 8 + 8, :] + acc_b[t, w * 8 : w * 8 + 8, :] for w in range(WEEKS)]
                scale = scale_ref[tc, pl.ds(tr, 1), :]
                ahead = [x[0]]
                for w in range(1, WEEKS):
                    ahead.append(x[w] + week_decay * ahead[-1])
                mixed = [None] * WEEKS
                mixed[WEEKS - 1] = ahead[WEEKS - 1]
                behind = week_decay * x[WEEKS - 1]
                for w in range(WEEKS - 2, -1, -1):
                    mixed[w] = ahead[w] + behind
                    behind = week_decay * (x[w] + behind)
                y = jnp.concatenate(mixed, axis=0) * scale
                hi = y.astype(jnp.bfloat16)
                hi_ref[tc, tr] = hi
                lo_ref[tc, tr] = (y - hi.astype(jnp.float32)).astype(jnp.bfloat16)
                if tc == 0:
                    edge = jnp.where(place == k, pltpu.roll(y, 4 * k, 1), edge)
                if tc == ACROSS - 1:
                    edge = jnp.where(place == k, pltpu.roll(y, (4 * k - 12) % 128, 1), edge)
            if tc == 0:
                west_ref[quad] = edge.astype(jnp.bfloat16)
            if tc == ACROSS - 1:
                east_ref[quad] = edge.astype(jnp.bfloat16)
            return carry

        lax.fori_loop(0, QUADS, finish, 0, unroll=2)
        top = hi_ref[tc, 0]
        bottom = hi_ref[tc, DOWN - 1]
        first_ref[tc] = jnp.where(even, bottom, top)
        second_ref[tc] = jnp.where(even, top, bottom)
        copies.append(pltpu.make_async_copy(hi_ref.at[tc], hi_hbm.at[tc], out_sem.at[0, tc]))
        copies.append(pltpu.make_async_copy(lo_ref.at[tc], lo_hbm.at[tc], out_sem.at[1, tc]))
        copies[-2].start()
        copies[-1].start()
    for copy in copies:
        copy.wait()


def receive_call(where, arrived, scale):
    vmem = pl.BlockSpec(memory_space=pltpu.VMEM)
    hbm = pl.BlockSpec(memory_space=pltpu.HBM)
    smem = pl.BlockSpec(memory_space=pltpu.SMEM)
    block = (ACROSS, DOWN, SLOT_ROWS, CELLS)
    row = jax.ShapeDtypeStruct((ACROSS, SLOT_ROWS, CELLS), jnp.bfloat16)
    column = jax.ShapeDtypeStruct((QUADS, SLOT_ROWS, CELLS), jnp.bfloat16)
    return pl.pallas_call(
        receive_kernel,
        out_shape=(
            pltpu.HBM(block, jnp.bfloat16),
            pltpu.HBM(block, jnp.bfloat16),
            row,
            row,
            column,
            column,
            jax.ShapeDtypeStruct((8, 128), jnp.int32),
        ),
        in_specs=[smem, vmem, vmem],
        out_specs=(hbm, hbm) + (vmem,) * 4 + (smem,),
        scratch_shapes=[
            pltpu.VMEM((TILES + 1, SLOT_ROWS, CELLS), jnp.float32),
            pltpu.VMEM((TILES + 1, SLOT_ROWS, CELLS), jnp.float32),
            pltpu.VMEM(block, jnp.bfloat16),
            pltpu.VMEM(block, jnp.bfloat16),
            pltpu.VMEM((8, 128), jnp.int32),
            pltpu.SemaphoreType.DMA,
            pltpu.SemaphoreType.DMA((2, ACROSS)),
        ],
        compiler_params=pltpu.CompilerParams(vmem_limit_bytes=24 * MIB),
        name="receive",
    )(where, arrived, scale)


def facing(flag, first, second):
    even = jnp.bitwise_and(flag, 1) == 0
    return jnp.where(even, first, second), jnp.where(even, second, first)


def corner_kernel(where_ref, first_ref, second_ref, west_ref, east_ref, first_out, second_out):
    lane = lax.broadcasted_iota(jnp.int32, (SLOT_ROWS, CELLS), 1)
    place = lax.shift_right_logical(jnp.bitwise_and(lane, 15), 2)
    even = jnp.bitwise_and(where_ref[1], 1) == 0

    def put(quad, west, east):
        first_out[quad] = jnp.where(even, east, west)
        second_out[quad] = jnp.where(even, west, east)

    for quad in range(QUADS):
        put(quad, west_ref[quad], east_ref[quad])
    corners = []
    for tc, shift in ((0, 0), (ACROSS - 1, 116)):
        below, above = facing(
            where_ref[0], first_ref[tc].astype(jnp.float32), second_ref[tc].astype(jnp.float32)
        )
        if shift:
            above = pltpu.roll(above, shift, 1)
        below = pltpu.roll(below, (shift + 4) % 128, 1)
        corners.append(jnp.where(place == 0, above, below).astype(jnp.bfloat16))
    put(QUADS, *corners)


def corner_call(where, first, second, west, east):
    vmem = pl.BlockSpec(memory_space=pltpu.VMEM)
    column = jax.ShapeDtypeStruct((QUADS + 1, SLOT_ROWS, CELLS), jnp.bfloat16)
    return pl.pallas_call(
        corner_kernel,
        out_shape=(column, column),
        in_specs=[pl.BlockSpec(memory_space=pltpu.SMEM)] + [vmem] * 4,
        out_specs=(vmem, vmem),
        compiler_params=pltpu.CompilerParams(vmem_limit_bytes=16 * MIB),
        name="corner",
    )(where, first, second, west, east)


def diffuse_kernel(
    where_ref, idx_ref, hi_hbm, lo_hbm, lat_first, lat_second, lon_first, lon_second,
    scale_ref, weight_hbm, mirror_hbm,
    inc_hbm, reply_hbm,
    hi_ref, lo_ref, inc_ref, half_ref, reply_ref, weight_ref, mirror_ref,
    reply_sem, const_sem, field_sem, inc_sem,
):
    lat, lon = where_ref[0], where_ref[1]
    last_row, last_col = DOWN + 1, ACROSS + 1

    def mirrored(block, side):
        rows = block.reshape(-1, CELLS)
        out = jnp.dot(rows, mirror_ref[side], preferred_element_type=jnp.float32)
        return out.astype(jnp.bfloat16).reshape(block.shape)

    fields = []
    for tc in range(ACROSS):
        fields.append(pltpu.make_async_copy(hi_hbm.at[tc], hi_ref.at[tc + 1, pl.ds(1, DOWN)], field_sem.at[0, tc]))
    for tc in range(ACROSS):
        fields.append(pltpu.make_async_copy(lo_hbm.at[tc], lo_ref.at[tc], field_sem.at[1, tc]))
    for copy in fields:
        copy.start()
    mirror_copy = pltpu.make_async_copy(mirror_hbm, mirror_ref, const_sem.at[0])
    mirror_copy.start()
    weight_copy = pltpu.make_async_copy(weight_hbm, weight_ref, const_sem.at[1])
    weight_copy.start()

    def unpack(i, one, two, k):
        east, west = facing(lon, one.astype(jnp.float32), two.astype(jnp.float32))
        hi_ref[0, i] = pltpu.roll(west, 12 - 4 * k, 1).astype(jnp.bfloat16)
        hi_ref[last_col, i] = (pltpu.roll(east, 128 - 4 * k, 1) if k else east).astype(jnp.bfloat16)

    def unpack_quad(quad, carry):
        for k in range(4):
            i = quad * 4 + k + 1
            unpack(i, lon_first[quad], lon_second[quad], k)
        return carry

    lax.fori_loop(0, QUADS, unpack_quad, 0, unroll=2)
    unpack(0, lon_first[QUADS], lon_second[QUADS], 0)
    unpack(last_row, lon_first[QUADS], lon_second[QUADS], 1)
    for tc in range(ACROSS):
        below, above = facing(lat, lat_first[tc], lat_second[tc])
        hi_ref[tc + 1, 0] = above
        hi_ref[tc + 1, last_row] = below
    mirror_copy.wait()
    for copy in fields[:ACROSS]:
        copy.wait()

    @pl.when(lat == 0)
    def _():
        for x in range(1, last_col):
            hi_ref[x, 0] = mirrored(hi_ref[x, 1], 0)

    @pl.when(lat == 3)
    def _():
        for x in range(1, last_col):
            hi_ref[x, last_row] = mirrored(hi_ref[x, DOWN], 1)

    @pl.when(lon == 0)
    def _():
        hi_ref[0] = mirrored(hi_ref[1], 2)

    @pl.when(lon == 31)
    def _():
        hi_ref[last_col] = mirrored(hi_ref[ACROSS], 3)

    @pl.when(lat == 0)
    def _():
        for x in (0, last_col):
            hi_ref[x, 0] = mirrored(hi_ref[x, 1], 0)

    @pl.when(lat == 3)
    def _():
        for x in (0, last_col):
            hi_ref[x, last_row] = mirrored(hi_ref[x, DOWN], 1)

    chunk = DIFFUSE_CHUNK
    lane = lax.broadcasted_iota(jnp.int32, (chunk * SLOT_ROWS, CELLS), 1)
    upper = lane < 64
    east_side = jnp.bitwise_and(lane, 15) < 8
    weight_copy.wait()

    stores = []
    for pair in range(ACROSS // 2):
        for part in range(DOWN // chunk):
            if pair == 0 and part == 0:
                for copy in fields[ACROSS:]:
                    copy.wait()

            def rows(x, start):
                return hi_ref[x, part * chunk + start : part * chunk + start + chunk].reshape(-1, CELLS)

            own = [rows(x, 1) for x in range(2 * pair, 2 * pair + 4)]
            both = [jnp.where(upper, rows(x, 2), rows(x, 0)) for x in range(2 * pair, 2 * pair + 4)]
            left = jnp.concatenate(
                [
                    own[1],
                    own[2],
                    jnp.where(east_side, own[3], own[0]),
                    both[1],
                    both[2],
                    jnp.where(east_side, both[3], both[0]),
                ],
                axis=1,
            )
            rest = [
                lo_ref[2 * pair + u, part * chunk : part * chunk + chunk].reshape(-1, CELLS) for u in range(2)
            ]
            total = jnp.dot(left, weight_ref[...], preferred_element_type=jnp.float32)
            total += jnp.dot(
                jnp.concatenate(rest, axis=1), weight_ref[:256], preferred_element_type=jnp.float32
            )
            for k in range(chunk):
                tr = part * chunk + k
                for u in range(2):
                    tc = 2 * pair + u
                    scale = scale_ref[tc, tr : tr + 1, :] * STEP_FACTOR
                    y = total[k * SLOT_ROWS : (k + 1) * SLOT_ROWS, u * 128 : (u + 1) * 128] * scale
                    inc_ref[tc, tr] = y
                    half_ref[tc * DOWN + tr] = y.astype(jnp.bfloat16)
            for tc in (2 * pair, 2 * pair + 1):
                block = pl.ds(part * chunk, chunk)
                stores.append(
                    pltpu.make_async_copy(inc_ref.at[tc, block], inc_hbm.at[tc, block], inc_sem.at[tc, part])
                )
                stores[-1].start()

    def answer(d, carry):
        reply_ref[d, :SLOT_ROWS, :] = half_ref[idx_ref[0, d]]
        reply_ref[d, SLOT_ROWS:, :] = half_ref[idx_ref[4, d]]
        return carry

    copies = []
    for k in range(4):
        lax.fori_loop(32 * k, 32 * k + 32, answer, 0, unroll=8)
        part = pl.ds(32 * k, 32)
        copies.append(pltpu.make_async_copy(reply_ref.at[part], reply_hbm.at[part], reply_sem.at[k]))
        copies[-1].start()
    for copy in stores + copies:
        copy.wait()


def diffuse_call(where, index, hi, lo, halos, scale, weight, mirror):
    vmem = pl.BlockSpec(memory_space=pltpu.VMEM)
    smem = pl.BlockSpec(memory_space=pltpu.SMEM)
    hbm = pl.BlockSpec(memory_space=pltpu.HBM)
    ringed = (ACROSS + 2, DOWN + 2, SLOT_ROWS, CELLS)
    block = (ACROSS, DOWN, SLOT_ROWS, CELLS)
    return pl.pallas_call(
        diffuse_kernel,
        out_shape=(pltpu.HBM(block, jnp.float32), pltpu.HBM((128, 2 * SLOT_ROWS, CELLS), jnp.bfloat16)),
        in_specs=[smem, smem, hbm, hbm] + [vmem] * 5 + [hbm] * 2,
        out_specs=(hbm, hbm),
        scratch_shapes=[
            pltpu.VMEM(ringed, jnp.bfloat16),
            pltpu.VMEM(block, jnp.bfloat16),
            pltpu.VMEM(block, jnp.float32),
            pltpu.VMEM((TILES + 1, SLOT_ROWS, CELLS), jnp.bfloat16),
            pltpu.VMEM((128, 2 * SLOT_ROWS, CELLS), jnp.bfloat16),
            pltpu.VMEM(weight.shape, weight.dtype),
            pltpu.VMEM(mirror.shape, mirror.dtype),
            pltpu.SemaphoreType.DMA((4,)),
            pltpu.SemaphoreType.DMA((2,)),
            pltpu.SemaphoreType.DMA((2, ACROSS)),
            pltpu.SemaphoreType.DMA((ACROSS, DOWN // DIFFUSE_CHUNK)),
        ],
        compiler_params=pltpu.CompilerParams(vmem_limit_bytes=32 * MIB),
        name="diffuse",
    )(where, index, in_hbm(hi), in_hbm(lo), *halos, scale, in_hbm(weight), in_hbm(mirror))


def layout_kernel(inc_ref, out_ref, rows_ref):
    lane = lax.broadcasted_iota(jnp.int32, (8, CELLS), 1)
    group = lax.shift_right_logical(lane, 4)

    def regroup(tr, carry):
        for half in range(2):
            v = [
                inc_ref[i % 4, tr, (half * 2 + i // 4) * 8 : (half * 2 + i // 4) * 8 + 8, :] for i in range(8)
            ]
            for bit in (1, 2, 4):
                clear = jnp.bitwise_and(group, bit) == 0
                for i in range(8):
                    if i & bit == 0:
                        a, c = v[i], v[i + bit]
                        v[i] = jnp.where(clear, a, pltpu.roll(c, 16 * bit, 1))
                        v[i + bit] = jnp.where(clear, pltpu.roll(a, 128 - 16 * bit, 1), c)
            for r in range(8):
                at = pl.multiple_of((half * 256 + tr * 8 + r) * 8, 8)
                rows_ref[pl.ds(at, 8), :] = v[r]
        return carry

    lax.fori_loop(0, DOWN, regroup, 0, unroll=2)

    for half in range(2):
        for p in range(PROBES):
            for k in range(2):
                block = rows_ref[pl.ds((half * 256 + k * 128) * 8 + p, 128, stride=8), :]
                out_ref[pl.ds((p * 4 + half * 2) * 64, 128), k * 128 : (k + 1) * 128] = block.T


def layout_call(inc):
    vmem = pl.BlockSpec(memory_space=pltpu.VMEM)
    return pl.pallas_call(
        layout_kernel,
        out_shape=jax.ShapeDtypeStruct((SLOT_ROWS * 64, 256), jnp.float32),
        in_specs=[vmem],
        out_specs=vmem,
        scratch_shapes=[pltpu.VMEM((2 * 256 * 8, CELLS), jnp.float32)],
        compiler_params=pltpu.CompilerParams(vmem_limit_bytes=16 * MIB),
        cost_estimate=pl.CostEstimate(flops=8 * MIB, bytes_accessed=8 * MIB, transcendentals=0),
        name="layout",
    )(inc)


def forward_kernel(pos_ref, tiles_ref, foot_hbm, out_ref, foot, foot_sem):
    groups, slots, sounds, span = foot.shape

    def fetch(g, first, last):
        part = (g, pl.ds(first, last - first))
        return pltpu.make_async_copy(foot_hbm.at[part], foot.at[part], foot_sem.at[g, first // LEAST])

    def start_group(g, carry):
        fetch(g, 0, LEAST).start()
        count = pos_ref[groups * slots + g]
        for n in range(LEAST + 1, slots + 1):

            @pl.when(count == n)
            def _():
                fetch(g, LEAST, n).start()

        return carry

    lax.fori_loop(0, groups, start_group, 0)

    def group(g, carry):
        def one(j):
            place = pos_ref[g * slots + j]
            at = pl.multiple_of(jnp.bitwise_and(place, 1) * SLOT_ROWS, SLOT_ROWS)
            tile = tiles_ref[lax.shift_right_logical(place, 1), pl.ds(at, SLOT_ROWS), :].astype(jnp.float32)
            left = jnp.concatenate([tile[w * 8 : w * 8 + 8] for w in range(WEEKS)], axis=1).astype(jnp.bfloat16)
            return lax.dot_general(
                left, foot[g, j], (((1,), (1,)), ((), ())), preferred_element_type=jnp.float32
            )

        count = pos_ref[groups * slots + g]
        for n in range(LEAST, slots + 1):

            @pl.when(count == n)
            def _():
                fetch(g, 0, LEAST).wait()
                if n > LEAST:
                    fetch(g, LEAST, n).wait()
                total = one(0)
                for j in range(1, n):
                    total = total + one(j)
                out_ref[g] = total

        return carry

    lax.fori_loop(0, groups, group, 0)


def forward_call(pos, tiles, footprints):
    groups, slots, sounds, span = footprints.shape
    smem = pl.BlockSpec(memory_space=pltpu.SMEM)
    vmem = pl.BlockSpec(memory_space=pltpu.VMEM)
    return pl.pallas_call(
        forward_kernel,
        out_shape=jax.ShapeDtypeStruct((groups, PROBES, sounds), jnp.float32),
        in_specs=[smem, vmem, pl.BlockSpec(memory_space=pltpu.HBM)],
        out_specs=vmem,
        scratch_shapes=[
            pltpu.VMEM(footprints.shape, footprints.dtype),
            pltpu.SemaphoreType.DMA((groups, 2)),
        ],
        compiler_params=pltpu.CompilerParams(vmem_limit_bytes=32 * MIB),
        name="forward",
    )(pos, tiles, in_hbm(footprints))


def exchanged(block):
    return lax.all_to_all(block, ("lat", "lon"), split_axis=0, concat_axis=0, tiled=True)


def swaps(count, start):
    lower = [(i, i + 1) for i in range(start, count - 1, 2)]
    return lower + [(j, i) for i, j in lower]


def per_device(
    footprints, tile_lists, tile_counts, tile_place, probes, obs_precision, prior_sigma, land_mask
):
    lat, lon = lax.axis_index("lat"), lax.axis_index("lon")
    outgoing, pos = adjoint_call(tile_lists, tile_counts, tile_place, probes, obs_precision, footprints)
    arrived = exchanged(outgoing)

    scale = prior_sigma * land_mask.astype(jnp.float32)
    scale = scale.reshape(DOWN, TILE_ROWS, ACROSS, TILE_COLS).transpose(2, 0, 1, 3).reshape(ACROSS, DOWN, CELLS)

    where = jnp.stack([lat, lon]).astype(jnp.int32)
    hi, lo, lat_one, lat_two, left, right, index = receive_call(where, arrived, scale)
    lat_one = lax.ppermute(lat_one, "lat", swaps(4, 0))
    lat_two = lax.ppermute(lat_two, "lat", swaps(4, 1))
    lon_one, lon_two = corner_call(where, lat_one, lat_two, left, right)
    lon_one = lax.ppermute(lon_one, "lon", swaps(32, 0))
    lon_two = lax.ppermute(lon_two, "lon", swaps(32, 1))
    halos = (lat_one, lat_two, lon_one, lon_two)

    weight = jnp.asarray(stencil_weights(), jnp.bfloat16)
    mirror = jnp.asarray(reflections(), jnp.bfloat16)
    inc, reply = diffuse_call(where, index, hi, lo, halos, scale, weight, mirror)
    returned = exchanged(reply)
    increment = layout_call(inc).reshape(SLOT_ROWS, 64, 256).transpose(2, 0, 1)
    predicted = forward_call(pos, returned, footprints)
    return (predicted, increment)


def solution(mesh):
    in_specs = (
        P(("lat", "lon"), None, None, None),
        P(("lat", "lon"), None),
        P(("lat", "lon")),
        P(),
        P(("lat", "lon"), None, None),
        P(("lat", "lon"), None),
        P("lat", "lon"),
        P("lat", "lon"),
    )
    out_specs = (P(("lat", "lon"), None, None), P("lat", None, "lon"))
    return jax.shard_map(
        per_device, mesh=mesh, in_specs=in_specs, out_specs=out_specs, check_vma=False
    )
```

```python
import functools

import jax
import jax.numpy as jnp
import numpy as np
from jax import lax
from jax.experimental import pallas as pl
from jax.experimental.pallas import tpu as pltpu
from jax.sharding import PartitionSpec as P

TILE_ROWS = 8
TILE_COLS = 16
WEEKS = 4
PROBES = 8
NSTEP = 4
CELLS = 128
SLOT_ROWS = WEEKS * PROBES
DOWN = 32
ACROSS = 4
TILES = DOWN * ACROSS
SEND_ROWS = 2 * SLOT_ROWS + 8
QUADS = DOWN // 4
DIFFUSE_CHUNK = 8
LEAST = 6

diffusion_rate = 0.2
week_decay = 0.6
MIB = 1 << 20

STEP_FACTOR = diffusion_rate**NSTEP


def stencil_coefficients():
    out = np.zeros((9, 9), np.int64)
    out[4, 4] = 1
    for _ in range(NSTEP):
        padded = np.pad(out, 1)
        out = (
            padded[1:-1, 1:-1]
            + padded[2:, 1:-1]
            + padded[:-2, 1:-1]
            + padded[1:-1, 2:]
            + padded[1:-1, :-2]
        )
    return out


def stencil_weights():
    coef = stencil_coefficients()
    lane = np.arange(128)
    r, c = lane // 16, lane % 16
    rows_own = r
    rows_ns = np.where(r < 4, 8 + r, r - 8)
    cols_ew = np.where(c < 8, 32 + c, c - 16)
    row_in = np.concatenate([rows_own] * 3 + [rows_ns] * 3)
    col_in = np.concatenate([c, 16 + c, cols_ew] * 2)
    row_out = np.concatenate([r, r])
    col_out = np.concatenate([c, 16 + c])
    dr = row_in[:, None] - row_out[None, :]
    dc = col_in[:, None] - col_out[None, :]
    near = (np.abs(dr) <= 4) & (np.abs(dc) <= 4)
    return np.where(near, coef[np.clip(dr + 4, 0, 8), np.clip(dc + 4, 0, 8)], 0).astype(np.float32)


def reflections():
    out = np.zeros((4, 128, 128), np.float32)
    for k in range(1, 4):
        for c in range(16):
            out[0, (k - 1) * 16 + c, (7 - k) * 16 + c] = -1
            out[1, (8 - k) * 16 + c, k * 16 + c] = -1
        for r in range(8):
            out[2, r * 16 + k - 1, r * 16 + 15 - k] = -1
            out[3, r * 16 + 16 - k, r * 16 + k] = -1
    return out


def in_hbm(x):
    return pltpu.with_memory_space_constraint(x, pltpu.HBM)


def adjoint_kernel(
    list_hbm, count_hbm, place_hbm, probe_hbm, prec_hbm, foot_hbm, out_hbm, pos_hbm,
    foot, packed, probe_ref, prec_ref, pos_ref, list_ref, count_ref, place_ref, seen_ref, small_sem, foot_sem, out_sem, pos_sem,
):
    groups, slots = foot.shape[:2]

    small = [
        pltpu.make_async_copy(src, dst, small_sem.at[k])
        for k, (src, dst) in enumerate(
            (
                (count_hbm, count_ref),
                (list_hbm, list_ref),
                (place_hbm, place_ref),
                (probe_hbm, probe_ref),
                (prec_hbm, prec_ref),
            )
        )
    ]
    for copy in small:
        copy.start()

    def fetch(g, first, last):
        part = (g, pl.ds(first, last - first))
        return pltpu.make_async_copy(foot_hbm.at[part], foot.at[part], foot_sem.at[g, first // LEAST])

    def start_sure(g, carry):
        fetch(g, 0, LEAST).start()
        return carry

    def start_rest(g, carry):
        count = count_ref[g]
        for n in range(LEAST + 1, slots + 1):

            @pl.when(count == n)
            def _():
                fetch(g, LEAST, n).start()

        return carry

    start_sure(0, 0)
    small[0].wait()
    start_rest(0, 0)

    def start_group(g, carry):
        start_sure(g, carry)
        return start_rest(g, carry)

    lax.fori_loop(1, groups, start_group, 0)

    nobody = jnp.full((8, CELLS), TILES, jnp.float32).astype(jnp.bfloat16)
    number_row = lax.shift_right_logical(lax.broadcasted_iota(jnp.int32, (8, CELLS), 0), 2)

    def clear(i, carry):
        seen_ref[i] = 0
        packed[i, 2 * SLOT_ROWS :, :] = nobody
        return carry

    lax.fori_loop(0, 128, clear, 0, unroll=8)
    for copy in small[1:]:
        copy.wait()

    def group(g, carry):
        count = count_ref[g]
        weighted = (prec_ref[pl.ds(g, 1), :] * probe_ref[g]).astype(jnp.bfloat16)

        def route(j):
            t = place_ref[list_ref[g, j]]
            row = lax.shift_right_logical(t, 7)
            col = jnp.bitwise_and(t, 127)
            owner = lax.shift_right_logical(row, 5) * 32 + lax.shift_right_logical(col, 2)
            local = jnp.bitwise_and(col, 3) * DOWN + jnp.bitwise_and(row, 31)
            rank = jnp.minimum(seen_ref[owner], 1)
            seen_ref[owner] = rank + 1
            pos_ref[g * slots + j] = owner * 2 + rank
            return owner, rank, local

        def slot(j):
            part = jnp.dot(weighted, foot[g, j], preferred_element_type=jnp.float32)
            owner, rank, local = route(j)
            part = jnp.concatenate([part[:, w * CELLS : (w + 1) * CELLS] for w in range(WEEKS)], axis=0)
            at = pl.multiple_of(rank * SLOT_ROWS, SLOT_ROWS)
            packed[owner, pl.ds(at, SLOT_ROWS), :] = part.astype(jnp.bfloat16)
            numbers = packed[owner, 2 * SLOT_ROWS :, :].astype(jnp.float32)
            numbers = jnp.where(number_row == rank, local.astype(jnp.float32), numbers)
            packed[owner, 2 * SLOT_ROWS :, :] = numbers.astype(jnp.bfloat16)

        for n in range(LEAST, slots + 1):

            @pl.when(count == n)
            def _():
                fetch(g, 0, LEAST).wait()
                if n > LEAST:
                    fetch(g, LEAST, n).wait()
                for j in range(n):
                    slot(j)
                for j in range(n, slots):
                    pos_ref[g * slots + j] = 0
                pos_ref[groups * slots + g] = n

        return carry

    lax.fori_loop(0, groups, group, 0)

    copies = [pltpu.make_async_copy(pos_ref, pos_hbm, pos_sem)]
    copies[0].start()
    for k in range(4):
        part = pl.ds(32 * k, 32)
        copies.append(pltpu.make_async_copy(packed.at[part], out_hbm.at[part], out_sem.at[k]))
        copies[-1].start()
    for copy in copies:
        copy.wait()


def adjoint_call(tile_lists, counts, tile_place, probes, precision, footprints):
    groups, slots, sounds, span = footprints.shape
    hbm = pl.BlockSpec(memory_space=pltpu.HBM)
    return pl.pallas_call(
        adjoint_kernel,
        out_shape=(
            pltpu.HBM((128, SEND_ROWS, CELLS), jnp.bfloat16),
            pltpu.HBM((groups * slots + groups,), jnp.int32),
        ),
        in_specs=[hbm] * 6,
        out_specs=(hbm, hbm),
        scratch_shapes=[
            pltpu.VMEM((groups, slots, sounds, span), jnp.bfloat16),
            pltpu.VMEM((128, SEND_ROWS, CELLS), jnp.bfloat16),
            pltpu.VMEM(probes.shape, probes.dtype),
            pltpu.VMEM(precision.shape, precision.dtype),
            pltpu.SMEM((groups * slots + groups,), jnp.int32),
            pltpu.SMEM(tile_lists.shape, jnp.int32),
            pltpu.SMEM(counts.shape, jnp.int32),
            pltpu.SMEM(tile_place.shape, jnp.int32),
            pltpu.SMEM((128,), jnp.int32),
            pltpu.SemaphoreType.DMA((5,)),
            pltpu.SemaphoreType.DMA((groups, 2)),
            pltpu.SemaphoreType.DMA((4,)),
            pltpu.SemaphoreType.DMA,
        ],
        compiler_params=pltpu.CompilerParams(vmem_limit_bytes=32 * MIB),
        name="adjoint",
    )(*map(in_hbm, (tile_lists, counts, tile_place, probes, precision, footprints)))


def receive_kernel(
    arr_ref, scale_ref, hi_hbm, lo_hbm, first_ref, second_ref, west_ref, east_ref, idx_vec,
    acc_a, acc_b, hi_ref, lo_ref, idx_ref, idx_sem, out_sem,
):
    zero = jnp.zeros((SLOT_ROWS, CELLS), jnp.float32)
    lane8 = lax.broadcasted_iota(jnp.int32, (8, CELLS), 1)

    def gather(d, found):
        return jnp.where(lane8 == d, arr_ref[d, 64:72, :].astype(jnp.float32), found)

    found = lax.fori_loop(0, 128, gather, jnp.zeros((8, CELLS), jnp.float32), unroll=16)
    idx_vec[...] = found.astype(jnp.int32)
    idx_copy = pltpu.make_async_copy(idx_vec, idx_ref, idx_sem)
    idx_copy.start()

    def clear(i, carry):
        acc_a[i] = zero
        acc_b[i] = zero
        return carry

    lax.fori_loop(0, TILES, clear, 0, unroll=8)
    idx_copy.wait()

    def add(d, carry):
        ia = idx_ref[0, d]
        ib = idx_ref[4, d]
        acc_a[ia] += arr_ref[d, :SLOT_ROWS, :].astype(jnp.float32)
        acc_b[ib] += arr_ref[d, SLOT_ROWS : 2 * SLOT_ROWS, :].astype(jnp.float32)
        return carry

    lax.fori_loop(0, 128, add, 0, unroll=8)

    lane = lax.broadcasted_iota(jnp.int32, (SLOT_ROWS, CELLS), 1)
    place = lax.shift_right_logical(jnp.bitwise_and(lane, 15), 2)

    copies = []
    even = jnp.bitwise_and(lax.axis_index("lat"), 1) == 0
    for tc in (1, 2, 0, 3):

        def finish(quad, carry):
            edge = zero
            for k in range(4):
                tr = quad * 4 + k
                t = tc * DOWN + tr
                x = [acc_a[t, w * 8 : w * 8 + 8, :] + acc_b[t, w * 8 : w * 8 + 8, :] for w in range(WEEKS)]
                scale = scale_ref[tc, pl.ds(tr, 1), :]
                ahead = [x[0]]
                for w in range(1, WEEKS):
                    ahead.append(x[w] + week_decay * ahead[-1])
                mixed = [None] * WEEKS
                mixed[WEEKS - 1] = ahead[WEEKS - 1]
                behind = week_decay * x[WEEKS - 1]
                for w in range(WEEKS - 2, -1, -1):
                    mixed[w] = ahead[w] + behind
                    behind = week_decay * (x[w] + behind)
                y = jnp.concatenate(mixed, axis=0) * scale
                hi = y.astype(jnp.bfloat16)
                hi_ref[tc, tr] = hi
                lo_ref[tc, tr] = (y - hi.astype(jnp.float32)).astype(jnp.bfloat16)
                if tc == 0:
                    edge = jnp.where(place == k, pltpu.roll(y, 4 * k, 1), edge)
                if tc == ACROSS - 1:
                    edge = jnp.where(place == k, pltpu.roll(y, (4 * k - 12) % 128, 1), edge)
            if tc == 0:
                west_ref[quad] = edge.astype(jnp.bfloat16)
            if tc == ACROSS - 1:
                east_ref[quad] = edge.astype(jnp.bfloat16)
            return carry

        lax.fori_loop(0, QUADS, finish, 0, unroll=2)
        top = hi_ref[tc, 0]
        bottom = hi_ref[tc, DOWN - 1]
        first_ref[tc] = jnp.where(even, bottom, top)
        second_ref[tc] = jnp.where(even, top, bottom)
        copies.append(pltpu.make_async_copy(hi_ref.at[tc], hi_hbm.at[tc], out_sem.at[0, tc]))
        copies.append(pltpu.make_async_copy(lo_ref.at[tc], lo_hbm.at[tc], out_sem.at[1, tc]))
        copies[-2].start()
        copies[-1].start()
    for copy in copies:
        copy.wait()


def receive_call(arrived, scale):
    vmem = pl.BlockSpec(memory_space=pltpu.VMEM)
    hbm = pl.BlockSpec(memory_space=pltpu.HBM)
    block = (ACROSS, DOWN, SLOT_ROWS, CELLS)
    row = jax.ShapeDtypeStruct((ACROSS, SLOT_ROWS, CELLS), jnp.bfloat16)
    column = jax.ShapeDtypeStruct((QUADS, SLOT_ROWS, CELLS), jnp.bfloat16)
    return pl.pallas_call(
        receive_kernel,
        out_shape=(
            pltpu.HBM(block, jnp.bfloat16),
            pltpu.HBM(block, jnp.bfloat16),
            row,
            row,
            column,
            column,
            jax.ShapeDtypeStruct((8, 128), jnp.int32),
        ),
        in_specs=[vmem, vmem],
        out_specs=(hbm, hbm) + (vmem,) * 5,
        scratch_shapes=[
            pltpu.VMEM((TILES + 1, SLOT_ROWS, CELLS), jnp.float32),
            pltpu.VMEM((TILES + 1, SLOT_ROWS, CELLS), jnp.float32),
            pltpu.VMEM(block, jnp.bfloat16),
            pltpu.VMEM(block, jnp.bfloat16),
            pltpu.SMEM((8, 128), jnp.int32),
            pltpu.SemaphoreType.DMA,
            pltpu.SemaphoreType.DMA((2, ACROSS)),
        ],
        compiler_params=pltpu.CompilerParams(vmem_limit_bytes=24 * MIB),
        name="receive",
    )(arrived, scale)


def facing(flag, first, second):
    even = jnp.bitwise_and(flag, 1) == 0
    return jnp.where(even, first, second), jnp.where(even, second, first)


def corner_kernel(first_ref, second_ref, west_ref, east_ref, first_out, second_out):
    lane = lax.broadcasted_iota(jnp.int32, (SLOT_ROWS, CELLS), 1)
    place = lax.shift_right_logical(jnp.bitwise_and(lane, 15), 2)
    even = jnp.bitwise_and(lax.axis_index("lon"), 1) == 0

    def put(quad, west, east):
        first_out[quad] = jnp.where(even, east, west)
        second_out[quad] = jnp.where(even, west, east)

    for quad in range(QUADS):
        put(quad, west_ref[quad], east_ref[quad])
    corners = []
    for tc, shift in ((0, 0), (ACROSS - 1, 116)):
        below, above = facing(
            lax.axis_index("lat"), first_ref[tc].astype(jnp.float32), second_ref[tc].astype(jnp.float32)
        )
        if shift:
            above = pltpu.roll(above, shift, 1)
        below = pltpu.roll(below, (shift + 4) % 128, 1)
        corners.append(jnp.where(place == 0, above, below).astype(jnp.bfloat16))
    put(QUADS, *corners)


def corner_call(first, second, west, east):
    vmem = pl.BlockSpec(memory_space=pltpu.VMEM)
    column = jax.ShapeDtypeStruct((QUADS + 1, SLOT_ROWS, CELLS), jnp.bfloat16)
    return pl.pallas_call(
        corner_kernel,
        out_shape=(column, column),
        in_specs=[vmem] * 4,
        out_specs=(vmem, vmem),
        compiler_params=pltpu.CompilerParams(vmem_limit_bytes=16 * MIB),
        name="corner",
    )(first, second, west, east)


def diffuse_kernel(
    idx_vec, hi_hbm, lo_hbm, lat_first, lat_second, lon_first, lon_second,
    scale_ref, weight_hbm, mirror_hbm,
    inc_hbm, reply_hbm,
    hi_ref, lo_ref, inc_ref, half_ref, reply_ref, weight_ref, mirror_ref, idx_ref,
    idx_sem, reply_sem, const_sem, field_sem, inc_sem,
):
    lat, lon = lax.axis_index("lat"), lax.axis_index("lon")
    idx_copy = pltpu.make_async_copy(idx_vec, idx_ref, idx_sem)
    idx_copy.start()
    last_row, last_col = DOWN + 1, ACROSS + 1

    def mirrored(block, side):
        rows = block.reshape(-1, CELLS)
        out = jnp.dot(rows, mirror_ref[side], preferred_element_type=jnp.float32)
        return out.astype(jnp.bfloat16).reshape(block.shape)

    fields = []
    for tc in range(ACROSS):
        fields.append(pltpu.make_async_copy(hi_hbm.at[tc], hi_ref.at[tc + 1, pl.ds(1, DOWN)], field_sem.at[0, tc]))
    for tc in range(ACROSS):
        fields.append(pltpu.make_async_copy(lo_hbm.at[tc], lo_ref.at[tc], field_sem.at[1, tc]))
    for copy in fields:
        copy.start()
    mirror_copy = pltpu.make_async_copy(mirror_hbm, mirror_ref, const_sem.at[0])
    mirror_copy.start()
    weight_copy = pltpu.make_async_copy(weight_hbm, weight_ref, const_sem.at[1])
    weight_copy.start()

    def unpack(i, one, two, k):
        east, west = facing(lon, one.astype(jnp.float32), two.astype(jnp.float32))
        hi_ref[0, i] = pltpu.roll(west, 12 - 4 * k, 1).astype(jnp.bfloat16)
        hi_ref[last_col, i] = (pltpu.roll(east, 128 - 4 * k, 1) if k else east).astype(jnp.bfloat16)

    def unpack_quad(quad, carry):
        for k in range(4):
            i = quad * 4 + k + 1
            unpack(i, lon_first[quad], lon_second[quad], k)
        return carry

    lax.fori_loop(0, QUADS, unpack_quad, 0, unroll=2)
    unpack(0, lon_first[QUADS], lon_second[QUADS], 0)
    unpack(last_row, lon_first[QUADS], lon_second[QUADS], 1)
    for tc in range(ACROSS):
        below, above = facing(lat, lat_first[tc], lat_second[tc])
        hi_ref[tc + 1, 0] = above
        hi_ref[tc + 1, last_row] = below
    mirror_copy.wait()
    for copy in fields[:ACROSS]:
        copy.wait()

    @pl.when(lat == 0)
    def _():
        for x in range(1, last_col):
            hi_ref[x, 0] = mirrored(hi_ref[x, 1], 0)

    @pl.when(lat == 3)
    def _():
        for x in range(1, last_col):
            hi_ref[x, last_row] = mirrored(hi_ref[x, DOWN], 1)

    @pl.when(lon == 0)
    def _():
        hi_ref[0] = mirrored(hi_ref[1], 2)

    @pl.when(lon == 31)
    def _():
        hi_ref[last_col] = mirrored(hi_ref[ACROSS], 3)

    @pl.when(lat == 0)
    def _():
        for x in (0, last_col):
            hi_ref[x, 0] = mirrored(hi_ref[x, 1], 0)

    @pl.when(lat == 3)
    def _():
        for x in (0, last_col):
            hi_ref[x, last_row] = mirrored(hi_ref[x, DOWN], 1)

    chunk = DIFFUSE_CHUNK
    lane = lax.broadcasted_iota(jnp.int32, (chunk * SLOT_ROWS, CELLS), 1)
    upper = lane < 64
    east_side = jnp.bitwise_and(lane, 15) < 8
    weight_copy.wait()

    stores = []
    for pair in range(ACROSS // 2):
        for part in range(DOWN // chunk):
            if pair == 0 and part == 0:
                for copy in fields[ACROSS:]:
                    copy.wait()

            def rows(x, start):
                return hi_ref[x, part * chunk + start : part * chunk + start + chunk].reshape(-1, CELLS)

            own = [rows(x, 1) for x in range(2 * pair, 2 * pair + 4)]
            both = [jnp.where(upper, rows(x, 2), rows(x, 0)) for x in range(2 * pair, 2 * pair + 4)]
            left = jnp.concatenate(
                [
                    own[1],
                    own[2],
                    jnp.where(east_side, own[3], own[0]),
                    both[1],
                    both[2],
                    jnp.where(east_side, both[3], both[0]),
                ],
                axis=1,
            )
            rest = [
                lo_ref[2 * pair + u, part * chunk : part * chunk + chunk].reshape(-1, CELLS) for u in range(2)
            ]
            total = jnp.dot(left, weight_ref[...], preferred_element_type=jnp.float32)
            total += jnp.dot(
                jnp.concatenate(rest, axis=1), weight_ref[:256], preferred_element_type=jnp.float32
            )
            for k in range(chunk):
                tr = part * chunk + k
                for u in range(2):
                    tc = 2 * pair + u
                    scale = scale_ref[tc, tr : tr + 1, :] * STEP_FACTOR
                    y = total[k * SLOT_ROWS : (k + 1) * SLOT_ROWS, u * 128 : (u + 1) * 128] * scale
                    inc_ref[tc, tr] = y
                    half_ref[tc * DOWN + tr] = y.astype(jnp.bfloat16)
            for tc in (2 * pair, 2 * pair + 1):
                block = pl.ds(part * chunk, chunk)
                stores.append(
                    pltpu.make_async_copy(inc_ref.at[tc, block], inc_hbm.at[tc, block], inc_sem.at[tc, part])
                )
                stores[-1].start()

    idx_copy.wait()

    def answer(d, carry):
        reply_ref[d, :SLOT_ROWS, :] = half_ref[idx_ref[0, d]]
        reply_ref[d, SLOT_ROWS:, :] = half_ref[idx_ref[4, d]]
        return carry

    copies = []
    for k in range(4):
        lax.fori_loop(32 * k, 32 * k + 32, answer, 0, unroll=8)
        part = pl.ds(32 * k, 32)
        copies.append(pltpu.make_async_copy(reply_ref.at[part], reply_hbm.at[part], reply_sem.at[k]))
        copies[-1].start()
    for copy in stores + copies:
        copy.wait()


def diffuse_call(index, hi, lo, halos, scale, weight, mirror):
    vmem = pl.BlockSpec(memory_space=pltpu.VMEM)
    hbm = pl.BlockSpec(memory_space=pltpu.HBM)
    ringed = (ACROSS + 2, DOWN + 2, SLOT_ROWS, CELLS)
    block = (ACROSS, DOWN, SLOT_ROWS, CELLS)
    return pl.pallas_call(
        diffuse_kernel,
        out_shape=(pltpu.HBM(block, jnp.float32), pltpu.HBM((128, 2 * SLOT_ROWS, CELLS), jnp.bfloat16)),
        in_specs=[vmem, hbm, hbm] + [vmem] * 5 + [hbm] * 2,
        out_specs=(hbm, hbm),
        scratch_shapes=[
            pltpu.VMEM(ringed, jnp.bfloat16),
            pltpu.VMEM(block, jnp.bfloat16),
            pltpu.VMEM(block, jnp.float32),
            pltpu.VMEM((TILES + 1, SLOT_ROWS, CELLS), jnp.bfloat16),
            pltpu.VMEM((128, 2 * SLOT_ROWS, CELLS), jnp.bfloat16),
            pltpu.VMEM(weight.shape, weight.dtype),
            pltpu.VMEM(mirror.shape, mirror.dtype),
            pltpu.SMEM((8, 128), jnp.int32),
            pltpu.SemaphoreType.DMA,
            pltpu.SemaphoreType.DMA((4,)),
            pltpu.SemaphoreType.DMA((2,)),
            pltpu.SemaphoreType.DMA((2, ACROSS)),
            pltpu.SemaphoreType.DMA((ACROSS, DOWN // DIFFUSE_CHUNK)),
        ],
        compiler_params=pltpu.CompilerParams(vmem_limit_bytes=32 * MIB),
        name="diffuse",
    )(index, in_hbm(hi), in_hbm(lo), *halos, scale, in_hbm(weight), in_hbm(mirror))


def layout_kernel(inc_ref, out_ref, rows_ref):
    lane = lax.broadcasted_iota(jnp.int32, (8, CELLS), 1)
    group = lax.shift_right_logical(lane, 4)

    def regroup(tr, carry):
        for half in range(2):
            v = [
                inc_ref[i % 4, tr, (half * 2 + i // 4) * 8 : (half * 2 + i // 4) * 8 + 8, :] for i in range(8)
            ]
            for bit in (1, 2, 4):
                clear = jnp.bitwise_and(group, bit) == 0
                for i in range(8):
                    if i & bit == 0:
                        a, c = v[i], v[i + bit]
                        v[i] = jnp.where(clear, a, pltpu.roll(c, 16 * bit, 1))
                        v[i + bit] = jnp.where(clear, pltpu.roll(a, 128 - 16 * bit, 1), c)
            for r in range(8):
                at = pl.multiple_of((half * 256 + tr * 8 + r) * 8, 8)
                rows_ref[pl.ds(at, 8), :] = v[r]
        return carry

    lax.fori_loop(0, DOWN, regroup, 0, unroll=2)

    for half in range(2):
        for p in range(PROBES):
            for k in range(2):
                block = rows_ref[pl.ds((half * 256 + k * 128) * 8 + p, 128, stride=8), :]
                out_ref[pl.ds((p * 4 + half * 2) * 64, 128), k * 128 : (k + 1) * 128] = block.T


def layout_call(inc):
    vmem = pl.BlockSpec(memory_space=pltpu.VMEM)
    return pl.pallas_call(
        layout_kernel,
        out_shape=jax.ShapeDtypeStruct((SLOT_ROWS * 64, 256), jnp.float32),
        in_specs=[vmem],
        out_specs=vmem,
        scratch_shapes=[pltpu.VMEM((2 * 256 * 8, CELLS), jnp.float32)],
        compiler_params=pltpu.CompilerParams(vmem_limit_bytes=16 * MIB),
        cost_estimate=pl.CostEstimate(flops=8 * MIB, bytes_accessed=8 * MIB, transcendentals=0),
        name="layout",
    )(inc)


def forward_kernel(pos_hbm, tiles_ref, foot_hbm, out_ref, foot, pos_ref, pos_sem, foot_sem):
    groups, slots, sounds, span = foot.shape

    def fetch(g, first, last):
        part = (g, pl.ds(first, last - first))
        return pltpu.make_async_copy(foot_hbm.at[part], foot.at[part], foot_sem.at[g, first // LEAST])

    pos_copy = pltpu.make_async_copy(pos_hbm, pos_ref, pos_sem)
    pos_copy.start()
    fetch(0, 0, LEAST).start()
    fetch(1, 0, LEAST).start()
    pos_copy.wait()

    def start_group(g, carry):
        @pl.when(g > 1)
        def _():
            fetch(g, 0, LEAST).start()

        count = pos_ref[groups * slots + g]
        for n in range(LEAST + 1, slots + 1):

            @pl.when(count == n)
            def _():
                fetch(g, LEAST, n).start()

        return carry

    lax.fori_loop(0, groups, start_group, 0)

    def group(g, carry):
        def one(j):
            place = pos_ref[g * slots + j]
            at = pl.multiple_of(jnp.bitwise_and(place, 1) * SLOT_ROWS, SLOT_ROWS)
            tile = tiles_ref[lax.shift_right_logical(place, 1), pl.ds(at, SLOT_ROWS), :].astype(jnp.float32)
            left = jnp.concatenate([tile[w * 8 : w * 8 + 8] for w in range(WEEKS)], axis=1).astype(jnp.bfloat16)
            return lax.dot_general(
                left, foot[g, j], (((1,), (1,)), ((), ())), preferred_element_type=jnp.float32
            )

        count = pos_ref[groups * slots + g]
        for n in range(LEAST, slots + 1):

            @pl.when(count == n)
            def _():
                fetch(g, 0, LEAST).wait()
                if n > LEAST:
                    fetch(g, LEAST, n).wait()
                total = one(0)
                for j in range(1, n):
                    total = total + one(j)
                out_ref[g] = total

        return carry

    lax.fori_loop(0, groups, group, 0)


def forward_call(pos, tiles, footprints):
    groups, slots, sounds, span = footprints.shape
    hbm = pl.BlockSpec(memory_space=pltpu.HBM)
    vmem = pl.BlockSpec(memory_space=pltpu.VMEM)
    return pl.pallas_call(
        forward_kernel,
        out_shape=jax.ShapeDtypeStruct((groups, PROBES, sounds), jnp.float32),
        in_specs=[hbm, vmem, hbm],
        out_specs=vmem,
        scratch_shapes=[
            pltpu.VMEM(footprints.shape, footprints.dtype),
            pltpu.SMEM(pos.shape, jnp.int32),
            pltpu.SemaphoreType.DMA,
            pltpu.SemaphoreType.DMA((groups, 2)),
        ],
        compiler_params=pltpu.CompilerParams(vmem_limit_bytes=32 * MIB),
        name="forward",
    )(in_hbm(pos), tiles, in_hbm(footprints))


def exchanged(block):
    return lax.all_to_all(block, ("lat", "lon"), split_axis=0, concat_axis=0, tiled=True)


def swaps(count, start):
    lower = [(i, i + 1) for i in range(start, count - 1, 2)]
    return lower + [(j, i) for i, j in lower]


def per_device(
    footprints, tile_lists, tile_counts, tile_place, probes, obs_precision, prior_sigma, land_mask
):
    outgoing, pos = adjoint_call(tile_lists, tile_counts, tile_place, probes, obs_precision, footprints)
    arrived = exchanged(outgoing)

    scale = prior_sigma * land_mask.astype(jnp.float32)
    scale = scale.reshape(DOWN, TILE_ROWS, ACROSS, TILE_COLS).transpose(2, 0, 1, 3).reshape(ACROSS, DOWN, CELLS)

    hi, lo, lat_one, lat_two, left, right, index = receive_call(arrived, scale)
    lat_one = lax.ppermute(lat_one, "lat", swaps(4, 0))
    lat_two = lax.ppermute(lat_two, "lat", swaps(4, 1))
    lon_one, lon_two = corner_call(lat_one, lat_two, left, right)
    lon_one = lax.ppermute(lon_one, "lon", swaps(32, 0))
    lon_two = lax.ppermute(lon_two, "lon", swaps(32, 1))
    halos = (lat_one, lat_two, lon_one, lon_two)

    weight = jnp.asarray(stencil_weights(), jnp.bfloat16)
    mirror = jnp.asarray(reflections(), jnp.bfloat16)
    inc, reply = diffuse_call(index, hi, lo, halos, scale, weight, mirror)
    returned = exchanged(reply)
    increment = layout_call(inc).reshape(SLOT_ROWS, 64, 256).transpose(2, 0, 1)
    predicted = forward_call(pos, returned, footprints)
    return (predicted, increment)


def solution(mesh):
    in_specs = (
        P(("lat", "lon"), None, None, None),
        P(("lat", "lon"), None),
        P(("lat", "lon")),
        P(),
        P(("lat", "lon"), None, None),
        P(("lat", "lon"), None),
        P("lat", "lon"),
        P("lat", "lon"),
    )
    out_specs = (P(("lat", "lon"), None, None), P("lat", None, "lon"))
    return jax.shard_map(
        per_device, mesh=mesh, in_specs=in_specs, out_specs=out_specs, check_vma=False
    )
```

```python
import functools

import jax
import jax.numpy as jnp
import numpy as np
from jax import lax
from jax.experimental import pallas as pl
from jax.experimental.pallas import tpu as pltpu
from jax.sharding import PartitionSpec as P

TILE_ROWS = 8
TILE_COLS = 16
WEEKS = 4
PROBES = 8
NSTEP = 4
CELLS = 128
SLOT_ROWS = WEEKS * PROBES
DOWN = 32
ACROSS = 4
TILES = DOWN * ACROSS
SEND_ROWS = 2 * SLOT_ROWS + 8
QUADS = DOWN // 4
DIFFUSE_CHUNK = 8
AHEAD = 4
LEAST = 6

diffusion_rate = 0.2
week_decay = 0.6
MIB = 1 << 20

STEP_FACTOR = diffusion_rate**NSTEP


def stencil_coefficients():
    out = np.zeros((9, 9), np.int64)
    out[4, 4] = 1
    for _ in range(NSTEP):
        padded = np.pad(out, 1)
        out = (
            padded[1:-1, 1:-1]
            + padded[2:, 1:-1]
            + padded[:-2, 1:-1]
            + padded[1:-1, 2:]
            + padded[1:-1, :-2]
        )
    return out


def stencil_weights():
    coef = stencil_coefficients()
    lane = np.arange(128)
    r, c = lane // 16, lane % 16
    rows_own = r
    rows_ns = np.where(r < 4, 8 + r, r - 8)
    cols_ew = np.where(c < 8, 32 + c, c - 16)
    row_in = np.concatenate([rows_own] * 3 + [rows_ns] * 3)
    col_in = np.concatenate([c, 16 + c, cols_ew] * 2)
    row_out = np.concatenate([r, r])
    col_out = np.concatenate([c, 16 + c])
    dr = row_in[:, None] - row_out[None, :]
    dc = col_in[:, None] - col_out[None, :]
    near = (np.abs(dr) <= 4) & (np.abs(dc) <= 4)
    return np.where(near, coef[np.clip(dr + 4, 0, 8), np.clip(dc + 4, 0, 8)], 0).astype(np.float32)


def reflections():
    out = np.zeros((4, 128, 128), np.float32)
    for k in range(1, 4):
        for c in range(16):
            out[0, (k - 1) * 16 + c, (7 - k) * 16 + c] = -1
            out[1, (8 - k) * 16 + c, k * 16 + c] = -1
        for r in range(8):
            out[2, r * 16 + k - 1, r * 16 + 15 - k] = -1
            out[3, r * 16 + 16 - k, r * 16 + k] = -1
    return out


def in_hbm(x):
    return pltpu.with_memory_space_constraint(x, pltpu.HBM)


def adjoint_kernel(
    list_hbm, count_hbm, place_hbm, probe_hbm, prec_hbm, foot_hbm, out_hbm, pos_hbm,
    foot, packed, probe_ref, prec_ref, pos_ref, list_ref, count_ref, place_ref, seen_ref, small_sem, foot_sem, out_sem, pos_sem,
):
    groups, slots = foot.shape[:2]

    small = [
        pltpu.make_async_copy(src, dst, small_sem.at[k])
        for k, (src, dst) in enumerate(
            (
                (count_hbm, count_ref),
                (list_hbm, list_ref),
                (place_hbm, place_ref),
                (probe_hbm, probe_ref),
                (prec_hbm, prec_ref),
            )
        )
    ]
    for copy in small:
        copy.start()

    def fetch(g, first, last):
        part = (g, pl.ds(first, last - first))
        return pltpu.make_async_copy(foot_hbm.at[part], foot.at[part], foot_sem.at[g, first // LEAST])

    def start_sure(g, carry):
        fetch(g, 0, LEAST).start()
        return carry

    def start_rest(g, carry):
        count = count_ref[g]
        for n in range(LEAST + 1, slots + 1):

            @pl.when(count == n)
            def _():
                fetch(g, LEAST, n).start()

        return carry

    for g in range(AHEAD):
        start_sure(g, 0)
    small[0].wait()
    for g in range(AHEAD):
        start_rest(g, 0)

    def start_group(g, carry):
        start_sure(g, carry)
        return start_rest(g, carry)

    lax.fori_loop(AHEAD, groups, start_group, 0)

    nobody = jnp.full((8, CELLS), TILES, jnp.float32).astype(jnp.bfloat16)
    number_row = lax.shift_right_logical(lax.broadcasted_iota(jnp.int32, (8, CELLS), 0), 2)

    def clear(i, carry):
        seen_ref[i] = 0
        packed[i, 2 * SLOT_ROWS :, :] = nobody
        return carry

    lax.fori_loop(0, 128, clear, 0, unroll=8)
    for copy in small[1:]:
        copy.wait()

    def group(g, carry):
        count = count_ref[g]
        weighted = (prec_ref[pl.ds(g, 1), :] * probe_ref[g]).astype(jnp.bfloat16)

        def route(j):
            t = place_ref[list_ref[g, j]]
            row = lax.shift_right_logical(t, 7)
            col = jnp.bitwise_and(t, 127)
            owner = lax.shift_right_logical(row, 5) * 32 + lax.shift_right_logical(col, 2)
            local = jnp.bitwise_and(col, 3) * DOWN + jnp.bitwise_and(row, 31)
            rank = jnp.minimum(seen_ref[owner], 1)
            seen_ref[owner] = rank + 1
            pos_ref[g * slots + j] = owner * 2 + rank
            return owner, rank, local

        def slot(j):
            part = jnp.dot(weighted, foot[g, j], preferred_element_type=jnp.float32)
            owner, rank, local = route(j)
            part = jnp.concatenate([part[:, w * CELLS : (w + 1) * CELLS] for w in range(WEEKS)], axis=0)
            at = pl.multiple_of(rank * SLOT_ROWS, SLOT_ROWS)
            packed[owner, pl.ds(at, SLOT_ROWS), :] = part.astype(jnp.bfloat16)
            numbers = packed[owner, 2 * SLOT_ROWS :, :].astype(jnp.float32)
            numbers = jnp.where(number_row == rank, local.astype(jnp.float32), numbers)
            packed[owner, 2 * SLOT_ROWS :, :] = numbers.astype(jnp.bfloat16)

        for n in range(LEAST, slots + 1):

            @pl.when(count == n)
            def _():
                fetch(g, 0, LEAST).wait()
                if n > LEAST:
                    fetch(g, LEAST, n).wait()
                for j in range(n):
                    slot(j)
                for j in range(n, slots):
                    pos_ref[g * slots + j] = 0
                pos_ref[groups * slots + g] = n

        return carry

    lax.fori_loop(0, groups, group, 0)

    copies = [pltpu.make_async_copy(pos_ref, pos_hbm, pos_sem)]
    copies[0].start()
    for k in range(4):
        part = pl.ds(32 * k, 32)
        copies.append(pltpu.make_async_copy(packed.at[part], out_hbm.at[part], out_sem.at[k]))
        copies[-1].start()
    for copy in copies:
        copy.wait()


def adjoint_call(tile_lists, counts, tile_place, probes, precision, footprints):
    groups, slots, sounds, span = footprints.shape
    hbm = pl.BlockSpec(memory_space=pltpu.HBM)
    return pl.pallas_call(
        adjoint_kernel,
        out_shape=(
            pltpu.HBM((128, SEND_ROWS, CELLS), jnp.bfloat16),
            pltpu.HBM((groups * slots + groups,), jnp.int32),
        ),
        in_specs=[hbm] * 6,
        out_specs=(hbm, hbm),
        scratch_shapes=[
            pltpu.VMEM((groups, slots, sounds, span), jnp.bfloat16),
            pltpu.VMEM((128, SEND_ROWS, CELLS), jnp.bfloat16),
            pltpu.VMEM(probes.shape, probes.dtype),
            pltpu.VMEM(precision.shape, precision.dtype),
            pltpu.SMEM((groups * slots + groups,), jnp.int32),
            pltpu.SMEM(tile_lists.shape, jnp.int32),
            pltpu.SMEM(counts.shape, jnp.int32),
            pltpu.SMEM(tile_place.shape, jnp.int32),
            pltpu.SMEM((128,), jnp.int32),
            pltpu.SemaphoreType.DMA((5,)),
            pltpu.SemaphoreType.DMA((groups, 2)),
            pltpu.SemaphoreType.DMA((4,)),
            pltpu.SemaphoreType.DMA,
        ],
        compiler_params=pltpu.CompilerParams(vmem_limit_bytes=32 * MIB),
        name="adjoint",
    )(*map(in_hbm, (tile_lists, counts, tile_place, probes, precision, footprints)))


def receive_kernel(
    arr_ref, scale_ref, hi_hbm, lo_hbm, first_ref, second_ref, west_ref, east_ref, idx_vec,
    acc_a, acc_b, hi_ref, lo_ref, idx_ref, idx_sem, out_sem,
):
    zero = jnp.zeros((SLOT_ROWS, CELLS), jnp.float32)
    lane8 = lax.broadcasted_iota(jnp.int32, (8, CELLS), 1)

    def gather(d, found):
        return jnp.where(lane8 == d, arr_ref[d, 64:72, :].astype(jnp.float32), found)

    found = lax.fori_loop(0, 128, gather, jnp.zeros((8, CELLS), jnp.float32), unroll=16)
    idx_vec[...] = found.astype(jnp.int32)
    idx_copy = pltpu.make_async_copy(idx_vec, idx_ref, idx_sem)
    idx_copy.start()

    def clear(i, carry):
        acc_a[i] = zero
        acc_b[i] = zero
        return carry

    lax.fori_loop(0, TILES, clear, 0, unroll=8)
    idx_copy.wait()

    def add(d, carry):
        ia = idx_ref[0, d]
        ib = idx_ref[4, d]
        acc_a[ia] += arr_ref[d, :SLOT_ROWS, :].astype(jnp.float32)
        acc_b[ib] += arr_ref[d, SLOT_ROWS : 2 * SLOT_ROWS, :].astype(jnp.float32)
        return carry

    lax.fori_loop(0, 128, add, 0, unroll=16)

    lane = lax.broadcasted_iota(jnp.int32, (SLOT_ROWS, CELLS), 1)
    place = lax.shift_right_logical(jnp.bitwise_and(lane, 15), 2)

    copies = []
    even = jnp.bitwise_and(lax.axis_index("lat"), 1) == 0
    for tc in (1, 2, 0, 3):

        def finish(quad, carry):
            edge = zero
            for k in range(4):
                tr = quad * 4 + k
                t = tc * DOWN + tr
                x = [acc_a[t, w * 8 : w * 8 + 8, :] + acc_b[t, w * 8 : w * 8 + 8, :] for w in range(WEEKS)]
                scale = scale_ref[tc, pl.ds(tr, 1), :]
                ahead = [x[0]]
                for w in range(1, WEEKS):
                    ahead.append(x[w] + week_decay * ahead[-1])
                mixed = [None] * WEEKS
                mixed[WEEKS - 1] = ahead[WEEKS - 1]
                behind = week_decay * x[WEEKS - 1]
                for w in range(WEEKS - 2, -1, -1):
                    mixed[w] = ahead[w] + behind
                    behind = week_decay * (x[w] + behind)
                y = jnp.concatenate(mixed, axis=0) * scale
                hi = y.astype(jnp.bfloat16)
                hi_ref[tc, tr] = hi
                lo_ref[tc, tr] = (y - hi.astype(jnp.float32)).astype(jnp.bfloat16)
                if tc == 0:
                    edge = jnp.where(place == k, pltpu.roll(y, 4 * k, 1), edge)
                if tc == ACROSS - 1:
                    edge = jnp.where(place == k, pltpu.roll(y, (4 * k - 12) % 128, 1), edge)
            if tc == 0:
                west_ref[quad] = edge.astype(jnp.bfloat16)
            if tc == ACROSS - 1:
                east_ref[quad] = edge.astype(jnp.bfloat16)
            return carry

        lax.fori_loop(0, QUADS, finish, 0, unroll=4)
        top = hi_ref[tc, 0]
        bottom = hi_ref[tc, DOWN - 1]
        first_ref[tc] = jnp.where(even, bottom, top)
        second_ref[tc] = jnp.where(even, top, bottom)
        copies.append(pltpu.make_async_copy(hi_ref.at[tc], hi_hbm.at[tc], out_sem.at[0, tc]))
        copies.append(pltpu.make_async_copy(lo_ref.at[tc], lo_hbm.at[tc], out_sem.at[1, tc]))
        copies[-2].start()
        copies[-1].start()
    for copy in copies:
        copy.wait()


def receive_call(arrived, scale):
    vmem = pl.BlockSpec(memory_space=pltpu.VMEM)
    hbm = pl.BlockSpec(memory_space=pltpu.HBM)
    block = (ACROSS, DOWN, SLOT_ROWS, CELLS)
    row = jax.ShapeDtypeStruct((ACROSS, SLOT_ROWS, CELLS), jnp.bfloat16)
    column = jax.ShapeDtypeStruct((QUADS, SLOT_ROWS, CELLS), jnp.bfloat16)
    return pl.pallas_call(
        receive_kernel,
        out_shape=(
            pltpu.HBM(block, jnp.bfloat16),
            pltpu.HBM(block, jnp.bfloat16),
            row,
            row,
            column,
            column,
            jax.ShapeDtypeStruct((8, 128), jnp.int32),
        ),
        in_specs=[vmem, vmem],
        out_specs=(hbm, hbm) + (vmem,) * 5,
        scratch_shapes=[
            pltpu.VMEM((TILES + 1, SLOT_ROWS, CELLS), jnp.float32),
            pltpu.VMEM((TILES + 1, SLOT_ROWS, CELLS), jnp.float32),
            pltpu.VMEM(block, jnp.bfloat16),
            pltpu.VMEM(block, jnp.bfloat16),
            pltpu.SMEM((8, 128), jnp.int32),
            pltpu.SemaphoreType.DMA,
            pltpu.SemaphoreType.DMA((2, ACROSS)),
        ],
        compiler_params=pltpu.CompilerParams(vmem_limit_bytes=24 * MIB),
        name="receive",
    )(arrived, scale)


def facing(flag, first, second):
    even = jnp.bitwise_and(flag, 1) == 0
    return jnp.where(even, first, second), jnp.where(even, second, first)


def corner_kernel(first_ref, second_ref, west_ref, east_ref, second_out, first_out):
    lane = lax.broadcasted_iota(jnp.int32, (SLOT_ROWS, CELLS), 1)
    place = lax.shift_right_logical(jnp.bitwise_and(lane, 15), 2)
    even = jnp.bitwise_and(lax.axis_index("lon"), 1) == 0

    def put(quad, west, east):
        first_out[quad] = jnp.where(even, east, west)
        second_out[quad] = jnp.where(even, west, east)

    for quad in range(QUADS):
        put(quad, west_ref[quad], east_ref[quad])
    corners = []
    for tc, shift in ((0, 0), (ACROSS - 1, 116)):
        below, above = facing(
            lax.axis_index("lat"), first_ref[tc].astype(jnp.float32), second_ref[tc].astype(jnp.float32)
        )
        if shift:
            above = pltpu.roll(above, shift, 1)
        below = pltpu.roll(below, (shift + 4) % 128, 1)
        corners.append(jnp.where(place == 0, above, below).astype(jnp.bfloat16))
    put(QUADS, *corners)


def corner_call(first, second, west, east):
    vmem = pl.BlockSpec(memory_space=pltpu.VMEM)
    column = jax.ShapeDtypeStruct((QUADS + 1, SLOT_ROWS, CELLS), jnp.bfloat16)
    return pl.pallas_call(
        corner_kernel,
        out_shape=(column, column),
        in_specs=[vmem] * 4,
        out_specs=(vmem, vmem),
        compiler_params=pltpu.CompilerParams(vmem_limit_bytes=16 * MIB),
        name="corner",
    )(first, second, west, east)


def diffuse_kernel(
    idx_vec, hi_hbm, lo_hbm, lat_first, lat_second, lon_second, lon_first,
    scale_ref, weight_hbm, mirror_hbm,
    inc_hbm, reply_hbm,
    hi_ref, lo_ref, inc_ref, half_ref, reply_ref, weight_ref, mirror_ref, idx_ref,
    idx_sem, reply_sem, const_sem, field_sem, inc_sem,
):
    lat, lon = lax.axis_index("lat"), lax.axis_index("lon")
    idx_copy = pltpu.make_async_copy(idx_vec, idx_ref, idx_sem)
    idx_copy.start()
    last_row, last_col = DOWN + 1, ACROSS + 1

    def mirrored(block, side):
        rows = block.reshape(-1, CELLS)
        out = jnp.dot(rows, mirror_ref[side], preferred_element_type=jnp.float32)
        return out.astype(jnp.bfloat16).reshape(block.shape)

    fields = []
    for tc in range(ACROSS):
        fields.append(pltpu.make_async_copy(hi_hbm.at[tc], hi_ref.at[tc + 1, pl.ds(1, DOWN)], field_sem.at[0, tc]))
    for tc in range(ACROSS):
        fields.append(pltpu.make_async_copy(lo_hbm.at[tc], lo_ref.at[tc], field_sem.at[1, tc]))
    for copy in fields:
        copy.start()
    mirror_copy = pltpu.make_async_copy(mirror_hbm, mirror_ref, const_sem.at[0])
    mirror_copy.start()
    weight_copy = pltpu.make_async_copy(weight_hbm, weight_ref, const_sem.at[1])
    weight_copy.start()

    def unpack(i, one, two, k):
        east, west = facing(lon, one.astype(jnp.float32), two.astype(jnp.float32))
        hi_ref[0, i] = pltpu.roll(west, 12 - 4 * k, 1).astype(jnp.bfloat16)
        hi_ref[last_col, i] = (pltpu.roll(east, 128 - 4 * k, 1) if k else east).astype(jnp.bfloat16)

    def unpack_quad(quad, carry):
        for k in range(4):
            i = quad * 4 + k + 1
            unpack(i, lon_first[quad], lon_second[quad], k)
        return carry

    lax.fori_loop(0, QUADS, unpack_quad, 0, unroll=4)
    unpack(0, lon_first[QUADS], lon_second[QUADS], 0)
    unpack(last_row, lon_first[QUADS], lon_second[QUADS], 1)
    for tc in range(ACROSS):
        below, above = facing(lat, lat_first[tc], lat_second[tc])
        hi_ref[tc + 1, 0] = above
        hi_ref[tc + 1, last_row] = below
    mirror_copy.wait()
    for copy in fields[:ACROSS]:
        copy.wait()

    @pl.when(lat == 0)
    def _():
        for x in range(1, last_col):
            hi_ref[x, 0] = mirrored(hi_ref[x, 1], 0)

    @pl.when(lat == 3)
    def _():
        for x in range(1, last_col):
            hi_ref[x, last_row] = mirrored(hi_ref[x, DOWN], 1)

    @pl.when(lon == 0)
    def _():
        hi_ref[0] = mirrored(hi_ref[1], 2)

    @pl.when(lon == 31)
    def _():
        hi_ref[last_col] = mirrored(hi_ref[ACROSS], 3)

    @pl.when(lat == 0)
    def _():
        for x in (0, last_col):
            hi_ref[x, 0] = mirrored(hi_ref[x, 1], 0)

    @pl.when(lat == 3)
    def _():
        for x in (0, last_col):
            hi_ref[x, last_row] = mirrored(hi_ref[x, DOWN], 1)

    chunk = DIFFUSE_CHUNK
    lane = lax.broadcasted_iota(jnp.int32, (chunk * SLOT_ROWS, CELLS), 1)
    upper = lane < 64
    east_side = jnp.bitwise_and(lane, 15) < 8
    weight_copy.wait()

    stores = []
    for pair in range(ACROSS // 2):
        for part in range(DOWN // chunk):
            if pair == 0 and part == 0:
                for copy in fields[ACROSS:]:
                    copy.wait()

            def rows(x, start):
                return hi_ref[x, part * chunk + start : part * chunk + start + chunk].reshape(-1, CELLS)

            own = [rows(x, 1) for x in range(2 * pair, 2 * pair + 4)]
            both = [jnp.where(upper, rows(x, 2), rows(x, 0)) for x in range(2 * pair, 2 * pair + 4)]
            left = jnp.concatenate(
                [
                    own[1],
                    own[2],
                    jnp.where(east_side, own[3], own[0]),
                    both[1],
                    both[2],
                    jnp.where(east_side, both[3], both[0]),
                ],
                axis=1,
            )
            rest = [
                lo_ref[2 * pair + u, part * chunk : part * chunk + chunk].reshape(-1, CELLS) for u in range(2)
            ]
            total = jnp.dot(left, weight_ref[...], preferred_element_type=jnp.float32)
            total += jnp.dot(
                jnp.concatenate(rest, axis=1), weight_ref[:256], preferred_element_type=jnp.float32
            )
            for k in range(chunk):
                tr = part * chunk + k
                for u in range(2):
                    tc = 2 * pair + u
                    scale = scale_ref[tc, tr : tr + 1, :] * STEP_FACTOR
                    y = total[k * SLOT_ROWS : (k + 1) * SLOT_ROWS, u * 128 : (u + 1) * 128] * scale
                    inc_ref[tc, tr] = y
                    half_ref[tc * DOWN + tr] = y.astype(jnp.bfloat16)
            for tc in (2 * pair, 2 * pair + 1):
                block = pl.ds(part * chunk, chunk)
                stores.append(
                    pltpu.make_async_copy(inc_ref.at[tc, block], inc_hbm.at[tc, block], inc_sem.at[tc, part])
                )
                stores[-1].start()

    idx_copy.wait()

    def answer(d, carry):
        reply_ref[d, :SLOT_ROWS, :] = half_ref[idx_ref[0, d]]
        reply_ref[d, SLOT_ROWS:, :] = half_ref[idx_ref[4, d]]
        return carry

    copies = []
    for k in range(4):
        lax.fori_loop(32 * k, 32 * k + 32, answer, 0, unroll=8)
        part = pl.ds(32 * k, 32)
        copies.append(pltpu.make_async_copy(reply_ref.at[part], reply_hbm.at[part], reply_sem.at[k]))
        copies[-1].start()
    for copy in stores + copies:
        copy.wait()


def diffuse_call(index, hi, lo, halos, scale, weight, mirror):
    vmem = pl.BlockSpec(memory_space=pltpu.VMEM)
    hbm = pl.BlockSpec(memory_space=pltpu.HBM)
    ringed = (ACROSS + 2, DOWN + 2, SLOT_ROWS, CELLS)
    block = (ACROSS, DOWN, SLOT_ROWS, CELLS)
    return pl.pallas_call(
        diffuse_kernel,
        out_shape=(pltpu.HBM(block, jnp.float32), pltpu.HBM((128, 2 * SLOT_ROWS, CELLS), jnp.bfloat16)),
        in_specs=[vmem, hbm, hbm] + [vmem] * 5 + [hbm] * 2,
        out_specs=(hbm, hbm),
        scratch_shapes=[
            pltpu.VMEM(ringed, jnp.bfloat16),
            pltpu.VMEM(block, jnp.bfloat16),
            pltpu.VMEM(block, jnp.float32),
            pltpu.VMEM((TILES + 1, SLOT_ROWS, CELLS), jnp.bfloat16),
            pltpu.VMEM((128, 2 * SLOT_ROWS, CELLS), jnp.bfloat16),
            pltpu.VMEM(weight.shape, weight.dtype),
            pltpu.VMEM(mirror.shape, mirror.dtype),
            pltpu.SMEM((8, 128), jnp.int32),
            pltpu.SemaphoreType.DMA,
            pltpu.SemaphoreType.DMA((4,)),
            pltpu.SemaphoreType.DMA((2,)),
            pltpu.SemaphoreType.DMA((2, ACROSS)),
            pltpu.SemaphoreType.DMA((ACROSS, DOWN // DIFFUSE_CHUNK)),
        ],
        compiler_params=pltpu.CompilerParams(vmem_limit_bytes=32 * MIB),
        name="diffuse",
    )(index, in_hbm(hi), in_hbm(lo), *halos, scale, in_hbm(weight), in_hbm(mirror))


def layout_kernel(inc_ref, out_ref, rows_ref):
    lane = lax.broadcasted_iota(jnp.int32, (8, CELLS), 1)
    group = lax.shift_right_logical(lane, 4)

    def regroup(tr, carry):
        for half in range(2):
            v = [
                inc_ref[i % 4, tr, (half * 2 + i // 4) * 8 : (half * 2 + i // 4) * 8 + 8, :] for i in range(8)
            ]
            for bit in (1, 2, 4):
                clear = jnp.bitwise_and(group, bit) == 0
                for i in range(8):
                    if i & bit == 0:
                        a, c = v[i], v[i + bit]
                        v[i] = jnp.where(clear, a, pltpu.roll(c, 16 * bit, 1))
                        v[i + bit] = jnp.where(clear, pltpu.roll(a, 128 - 16 * bit, 1), c)
            for r in range(8):
                at = pl.multiple_of((half * 256 + tr * 8 + r) * 8, 8)
                rows_ref[pl.ds(at, 8), :] = v[r]
        return carry

    lax.fori_loop(0, DOWN, regroup, 0, unroll=2)

    for half in range(2):
        for p in range(PROBES):
            for k in range(2):
                block = rows_ref[pl.ds((half * 256 + k * 128) * 8 + p, 128, stride=8), :]
                out_ref[pl.ds((p * 4 + half * 2) * 64, 128), k * 128 : (k + 1) * 128] = block.T


def layout_call(inc):
    vmem = pl.BlockSpec(memory_space=pltpu.VMEM)
    return pl.pallas_call(
        layout_kernel,
        out_shape=jax.ShapeDtypeStruct((SLOT_ROWS * 64, 256), jnp.float32),
        in_specs=[vmem],
        out_specs=vmem,
        scratch_shapes=[pltpu.VMEM((2 * 256 * 8, CELLS), jnp.float32)],
        compiler_params=pltpu.CompilerParams(vmem_limit_bytes=16 * MIB),
        cost_estimate=pl.CostEstimate(flops=8 * MIB, bytes_accessed=8 * MIB, transcendentals=0),
        name="layout",
    )(inc)


def forward_kernel(pos_hbm, tiles_ref, foot_hbm, out_ref, foot, pos_ref, pos_sem, foot_sem):
    groups, slots, sounds, span = foot.shape

    def fetch(g, first, last):
        part = (g, pl.ds(first, last - first))
        return pltpu.make_async_copy(foot_hbm.at[part], foot.at[part], foot_sem.at[g, first // LEAST])

    pos_copy = pltpu.make_async_copy(pos_hbm, pos_ref, pos_sem)
    pos_copy.start()
    for g in range(AHEAD):
        fetch(g, 0, LEAST).start()
    pos_copy.wait()

    def start_group(g, carry):
        @pl.when(g >= AHEAD)
        def _():
            fetch(g, 0, LEAST).start()

        count = pos_ref[groups * slots + g]
        for n in range(LEAST + 1, slots + 1):

            @pl.when(count == n)
            def _():
                fetch(g, LEAST, n).start()

        return carry

    lax.fori_loop(0, groups, start_group, 0)

    def group(g, carry):
        def one(j):
            place = pos_ref[g * slots + j]
            at = pl.multiple_of(jnp.bitwise_and(place, 1) * SLOT_ROWS, SLOT_ROWS)
            tile = tiles_ref[lax.shift_right_logical(place, 1), pl.ds(at, SLOT_ROWS), :].astype(jnp.float32)
            left = jnp.concatenate([tile[w * 8 : w * 8 + 8] for w in range(WEEKS)], axis=1).astype(jnp.bfloat16)
            return lax.dot_general(
                left, foot[g, j], (((1,), (1,)), ((), ())), preferred_element_type=jnp.float32
            )

        count = pos_ref[groups * slots + g]
        for n in range(LEAST, slots + 1):

            @pl.when(count == n)
            def _():
                fetch(g, 0, LEAST).wait()
                if n > LEAST:
                    fetch(g, LEAST, n).wait()
                total = one(0)
                for j in range(1, n):
                    total = total + one(j)
                out_ref[g] = total

        return carry

    lax.fori_loop(0, groups, group, 0)


def forward_call(pos, tiles, footprints):
    groups, slots, sounds, span = footprints.shape
    hbm = pl.BlockSpec(memory_space=pltpu.HBM)
    vmem = pl.BlockSpec(memory_space=pltpu.VMEM)
    return pl.pallas_call(
        forward_kernel,
        out_shape=jax.ShapeDtypeStruct((groups, PROBES, sounds), jnp.float32),
        in_specs=[hbm, vmem, hbm],
        out_specs=vmem,
        scratch_shapes=[
            pltpu.VMEM(footprints.shape, footprints.dtype),
            pltpu.SMEM(pos.shape, jnp.int32),
            pltpu.SemaphoreType.DMA,
            pltpu.SemaphoreType.DMA((groups, 2)),
        ],
        compiler_params=pltpu.CompilerParams(vmem_limit_bytes=32 * MIB),
        name="forward",
    )(in_hbm(pos), tiles, in_hbm(footprints))


def exchanged(block):
    return lax.all_to_all(block, ("lat", "lon"), split_axis=0, concat_axis=0, tiled=True)


def swaps(count, start):
    lower = [(i, i + 1) for i in range(start, count - 1, 2)]
    return lower + [(j, i) for i, j in lower]


def per_device(
    footprints, tile_lists, tile_counts, tile_place, probes, obs_precision, prior_sigma, land_mask
):
    outgoing, pos = adjoint_call(tile_lists, tile_counts, tile_place, probes, obs_precision, footprints)
    arrived = exchanged(outgoing)

    scale = prior_sigma * land_mask.astype(jnp.float32)
    scale = scale.reshape(DOWN, TILE_ROWS, ACROSS, TILE_COLS).transpose(2, 0, 1, 3).reshape(ACROSS, DOWN, CELLS)

    hi, lo, lat_one, lat_two, left, right, index = receive_call(arrived, scale)
    lat_one = lax.ppermute(lat_one, "lat", swaps(4, 0))
    lat_two = lax.ppermute(lat_two, "lat", swaps(4, 1))
    lon_two, lon_one = corner_call(lat_one, lat_two, left, right)
    lon_two = lax.ppermute(lon_two, "lon", swaps(32, 1))
    lon_one = lax.ppermute(lon_one, "lon", swaps(32, 0))
    halos = (lat_one, lat_two, lon_two, lon_one)

    weight = jnp.asarray(stencil_weights(), jnp.bfloat16)
    mirror = jnp.asarray(reflections(), jnp.bfloat16)
    inc, reply = diffuse_call(index, hi, lo, halos, scale, weight, mirror)
    returned = exchanged(reply)
    increment = layout_call(inc).reshape(SLOT_ROWS, 64, 256).transpose(2, 0, 1)
    predicted = forward_call(pos, returned, footprints)
    return (predicted, increment)


def solution(mesh):
    in_specs = (
        P(("lat", "lon"), None, None, None),
        P(("lat", "lon"), None),
        P(("lat", "lon")),
        P(),
        P(("lat", "lon"), None, None),
        P(("lat", "lon"), None),
        P("lat", "lon"),
        P("lat", "lon"),
    )
    out_specs = (P(("lat", "lon"), None, None), P("lat", None, "lon"))
    return jax.shard_map(
        per_device, mesh=mesh, in_specs=in_specs, out_specs=out_specs, check_vma=False
    )
```
